32 devices in a mesh: span: 4 (over z), stream: 8 (over y, x, core).
Axes of the slice: x: 2, y: 2, z: 4, core: 2. Of those that a mesh axis runs over, the one named last changes fastest.
Arguments:
- right_side: float32 [64, 65536], P(None, ('span', 'stream')), may hold values from -6 to 6
- start_guess: float32 [64, 65536], P(None, ('span', 'stream')), may hold values from -6 to 6
- fine_matrix: bfloat16 [512, 5, 128, 128], P(('span', 'stream'))
- fine_columns: int32 [512, 5], P(('span', 'stream')), may hold values from 0 to 31, as said below
- send_lists: int32 [32, 16], P(('span', 'stream')), may hold values from 0 to 15
- aggregates: int32 [65536], P(('span', 'stream')), may hold values from 0 to 127
- coarse_matrix: float32 [32, 5, 128, 128], P(('span', 'stream'))
Outputs:
- solution: float32 [64, 65536], P(None, ('span', 'stream'))
- coarse_correction: float32 [64, 4096], P(None, ('span', 'stream'))
The draws below stay inside these ranges and needn't reach their ends.
Inputs may be any that keep to these rules, and one draw needn't show every extreme that they name: `fine_columns`: entry 0 of each block row is the row block itself (its local index); the entries of one block row are distinct; entries below 16 name local blocks, entry 16 + d * 4 + h names received slot h from neighbour d; on every device every received slot is named by some block row.
All inputs are finite; a program needn't handle non-finite values.
Results may differ from the reference program's by a relative error of at most 0.0003.
Values sent between devices are 32-bit elements; how exact they have to be, the bound alone decides.
No kernel may reach another device: no remote copies, remote signals or barrier semaphores. Data moves between devices by JAX's collectives and lax.ppermute only.
A program may use at most 64 MiB of HBM per device.

```python
import jax
import jax.numpy as jnp
from jax import lax

BS = 128
RB = 16
NNZB = 5
HB = 4
NV = 64
ROWBLOCKS = 512
ROWS = 65536
CROWS = 4096
N_SPAN = 4
N_STREAM = 8
DEVICES = 32


def matrix_draw(key, shape, spread):
    key_noise, key_diag = jax.random.split(key, 2)
    noise = jnp.clip(jax.random.normal(key_noise, shape, jnp.float32), -4.0, 4.0)
    size_one = shape[2]
    inner = shape[1]
    same = jnp.arange(size_one)[:, None] == jnp.arange(size_one)[None, :]
    first = (jnp.arange(inner) == 0)[:, None, None]
    identity = jnp.logical_and(same[None, :, :], first).astype(jnp.float32)
    diag_values = 1.5 + 2.5 * jax.random.uniform(key_diag, (shape[0], 1, size_one, 1), jnp.float32)
    result = noise * spread + identity[None] * diag_values
    return result.astype(jnp.float32)


def draw_fine_matrix(key, part):
    return matrix_draw(key, (ROWBLOCKS, NNZB, BS, BS), 0.8 / (NNZB * BS) ** 0.5).astype(jnp.bfloat16)


def draw_coarse_matrix(key, part):
    return matrix_draw(key, (DEVICES, 5, BS, BS), 0.8 / (5 * BS) ** 0.5)


def device_columns(key):
    key_rows, key_rest = jax.random.split(key)
    row_order = jax.random.permutation(key_rows, RB).astype(jnp.int32)
    slot_of_row = jnp.full((RB,), -1, jnp.int32).at[row_order[:4 * HB]].set(jnp.arange(4 * HB, dtype=jnp.int32))
    row_keys = jax.random.split(key_rest, RB)
    perms = jax.vmap(lambda one: jax.random.permutation(one, RB - 1))(row_keys).astype(jnp.int32)
    rows = jnp.arange(RB, dtype=jnp.int32)
    others = (rows[:, None] + 1 + perms) % RB
    has_slot = slot_of_row >= 0
    leading = jnp.where(has_slot, RB + slot_of_row, others[:, 0])
    if NNZB > 2:
        trailing = jnp.where(has_slot[:, None], others[:, :NNZB - 2], others[:, 1:NNZB - 1])
        return jnp.concatenate([rows[:, None], leading[:, None], trailing], 1).astype(jnp.int32)
    return jnp.concatenate([rows[:, None], leading[:, None]], 1).astype(jnp.int32)


def draw_fine_columns(key, part):
    keys = jax.random.split(key, DEVICES)
    return jax.vmap(device_columns)(keys).reshape(ROWBLOCKS, NNZB).astype(jnp.int32)


def touch_ends(drawn, rng, least, largest):
    index_at = [jax.random.randint(jax.random.fold_in(rng, axis), (), 0, length) for axis, length in enumerate(drawn.shape)]
    longest = drawn.shape.index(max(drawn.shape))
    neighbour = index_at[:longest] + [(index_at[longest] + 1) % drawn.shape[longest]] + index_at[longest + 1:]
    return drawn.at[tuple(index_at)].set(least).at[tuple(neighbour)].set(largest)


def steps_of(key, extent, cuts, low, largest):
    level, own = 1.0, jax.random.fold_in(key, 6)
    for axis_at, blocks in cuts:
        draws = jnp.exp(jax.random.uniform(jax.random.fold_in(own, axis_at), (blocks,), jnp.float32, low / len(cuts), largest / len(cuts)))
        level = level * jnp.repeat(draws, extent[axis_at] // blocks).reshape([-1 if axis == axis_at else 1 for axis in range(len(extent))])
    return level


def bell_draw(key, dims, scale, bound, shards=(), kind=jnp.bfloat16):
    array = scale * jax.random.normal(key, dims, jnp.float32)
    if shards:
        array = array * steps_of(key, dims, shards, -0.22, 0.18)
    return jnp.clip(array, -bound, bound).astype(kind)


def setup_inputs(seed: int = 0) -> dict:
    key_list = jax.random.split(jax.random.key(seed), 8)
    return {
        "right_side": bell_draw(key_list[0], (NV, ROWS), 1.0, 6.0, ((1, 32),), jnp.float32),
        "start_guess": bell_draw(key_list[1], (NV, ROWS), 1.0, 6.0, ((1, 32),), jnp.float32),
        "fine_matrix": draw_fine_matrix(jax.random.fold_in(key_list[7], 71), 0),
        "fine_columns": draw_fine_columns(jax.random.fold_in(key_list[7], 71), 0),
        "send_lists": touch_ends(jax.random.randint(key_list[4], (DEVICES, 4 * HB), 0, RB), jax.random.fold_in(key_list[4], 1), 0, RB - 1).astype(jnp.int32),
        "aggregates": touch_ends(jax.random.randint(key_list[5], (ROWS,), 0, BS), jax.random.fold_in(key_list[5], 1), 0, BS - 1).astype(jnp.int32),
        "coarse_matrix": draw_coarse_matrix(jax.random.fold_in(key_list[7], 71), 0),
    }


center_value = 1.1
radius_value = 0.9
highest = lax.Precision.HIGHEST


def smooth(operator, inverse, target, start):
    if start is None:
        residual = target
        iterate = jnp.zeros_like(target)
    else:
        residual = target - operator(start)
        iterate = start
    update = inverse * residual / center_value
    iterate = iterate + update
    weight_old = radius_value / center_value
    for sweep in range(2):
        residual = residual - operator(update)
        weight_now = 1.0 / (2.0 * center_value / radius_value - weight_old)
        update = weight_now * weight_old * update + (2.0 * weight_now / radius_value) * inverse * residual
        iterate = iterate + update
        weight_old = weight_now
    return iterate


def neighbours():
    device = jnp.arange(DEVICES, dtype=jnp.int32)
    span_idx = device // N_STREAM
    stream_idx = device % N_STREAM
    near = jnp.stack([device - N_STREAM, device + N_STREAM, device - 1, device + 1], 1)
    valid = jnp.stack([span_idx > 0, span_idx < N_SPAN - 1, stream_idx > 0, stream_idx < N_STREAM - 1], 1)
    near = jnp.clip(near, 0, DEVICES - 1).astype(jnp.int32)
    return near, valid


def fine_operator(vector, fine_matrix, fine_columns, send_lists):
    near, valid = neighbours()
    blocks = vector.reshape(NV, DEVICES, RB, BS)
    lists = send_lists.reshape(DEVICES, 4, HB)
    parts = [blocks]
    for direction in range(4):
        source = near[:, direction]
        chosen = lists[source, direction ^ 1]
        got = blocks[:, source[:, None], chosen]
        parts.append(jnp.where(valid[:, direction][None, :, None, None], got, 0.0))
    extended = jnp.concatenate(parts, axis=2)
    group = 16 if DEVICES % 16 == 0 else 1
    index_all = fine_columns.reshape(DEVICES, RB * NNZB)
    mats = fine_matrix.reshape(DEVICES, RB, NNZB, BS, BS)

    def one_group(number):
        begin = (number * group).astype(jnp.int32)
        sub = lax.dynamic_slice_in_dim(extended, begin, group, axis=1)
        index = lax.dynamic_slice_in_dim(index_all, begin, group, axis=0)
        picked = jnp.take_along_axis(sub, index[None, :, :, None], axis=2)
        picked = picked.reshape(NV, group, RB, NNZB, BS)
        block_mats = lax.dynamic_slice_in_dim(mats, begin, group, axis=0).astype(jnp.float32)
        return jnp.einsum('grkij,vgrkj->gvri', block_mats, picked, precision=highest)

    result = lax.map(one_group, jnp.arange(DEVICES // group, dtype=jnp.int32))
    result = result.reshape(DEVICES, NV, RB, BS).transpose(1, 0, 2, 3)
    return result.reshape(NV, ROWS)


def coarse_operator(vector, coarse_matrix):
    near, valid = neighbours()
    blocks = vector.reshape(NV, DEVICES, BS)
    parts = [blocks]
    for direction in range(4):
        got = blocks[:, near[:, direction]]
        parts.append(jnp.where(valid[:, direction][None, :, None], got, 0.0))
    extended = jnp.stack(parts, axis=2)
    result = jnp.einsum('pkij,vpkj->vpi', coarse_matrix, extended, precision=highest)
    return result.reshape(NV, CROWS)


def reference(right_side, start_guess, fine_matrix, fine_columns, send_lists, aggregates, coarse_matrix):
    fine_inverse = 1.0 / jnp.diagonal(fine_matrix[:, 0], axis1=1, axis2=2).astype(jnp.float32).reshape(ROWS)
    coarse_inverse = 1.0 / jnp.diagonal(coarse_matrix[:, 0], axis1=1, axis2=2).reshape(CROWS)

    def fine_apply(vector):
        return fine_operator(vector, fine_matrix, fine_columns, send_lists)

    def coarse_apply(vector):
        return coarse_operator(vector, coarse_matrix)

    first = smooth(fine_apply, fine_inverse, right_side, start_guess)
    leftover = right_side - fine_apply(first)
    cell_ids = (jnp.arange(ROWS, dtype=jnp.int32) // (RB * BS)) * BS + aggregates.astype(jnp.int32)
    cell_ids = cell_ids.astype(jnp.int32)
    coarse_rhs = jax.ops.segment_sum(leftover.T, cell_ids, num_segments=CROWS).T
    correction = smooth(coarse_apply, coarse_inverse, coarse_rhs, None)
    second = first + correction[:, cell_ids]
    solution = smooth(fine_apply, fine_inverse, right_side, second)
    return (solution, correction)
```

```python
import functools

import jax
import jax.numpy as jnp
from jax import lax
from jax.experimental import pallas as pl
from jax.experimental.pallas import tpu as pltpu
from jax.sharding import PartitionSpec as P

center_value = 1.1
radius_value = 0.9
AXES = ("span", "stream")
CHUNK = 16
f32 = jnp.float32
bf16 = jnp.bfloat16


def chebyshev_weights():
    weights = []
    old = radius_value / center_value
    for _ in range(2):
        now = 1.0 / (2.0 * center_value / radius_value - old)
        weights.append((now * old, 2.0 * now / radius_value))
        old = now
    return weights


def even_partner(i, n):
    return i ^ 1 if (i ^ 1) < n else None


def odd_partner(i, n):
    j = ((i + 1) ^ 1) - 1
    return j if 0 <= j < n else None


def exchanges(n_span, n_stream):
    def flat(rule):
        return [
            (s * n_stream + t, rule(s, t)) for s in range(n_span) for t in range(n_stream)
        ]

    def along_span(rule):
        def pick(s, t):
            other = rule(s, n_span)
            if other is not None:
                return other * n_stream + t
            spare = even_partner(t, n_stream)
            return s * n_stream + (t if spare is None else spare)

        return pick

    def along_stream(rule):
        def pick(s, t):
            other = rule(t, n_stream)
            if other is not None:
                return s * n_stream + other
            spare = even_partner(s, n_span)
            return (s if spare is None else spare) * n_stream + t

        return pick

    return [
        flat(along_span(even_partner)),
        flat(along_span(odd_partner)),
        flat(along_stream(even_partner)),
        flat(along_stream(odd_partner)),
    ]


def dot_nt(a, b):
    return lax.dot_general(a, b, (((1,), (1,)), ((), ())), preferred_element_type=f32)


def dot_nn(a, b):
    return lax.dot_general(a, b, (((1,), (0,)), ((), ())), preferred_element_type=f32)


def high_low(x):
    high = x.astype(bf16)
    return high, (x - high.astype(f32)).astype(bf16)


def block(index, size):
    return pl.ds(pl.multiple_of(index * size, size), size)


def direction_of(meta, buffer):
    return buffer ^ meta[buffer // 2]


def pack(meta, lists, field, outs, size):
    slots = lists.shape[0] // 4
    rows = field.shape[0]
    for buffer in range(4):
        direction = direction_of(meta, buffer)
        for h in range(slots):
            source = lists[direction * slots + h]
            outs[buffer][0:rows, h * size : (h + 1) * size] = field[:, block(source, size)]


def pack_kernel(meta, lists, field, groups, *outs, size):
    slots = lists.shape[0] // 4
    rows = field.shape[0]
    pack(meta, lists, field, outs, size)
    for buffer in range(4):
        direction = direction_of(meta, buffer)
        for h in range(slots):
            source = lists[direction * slots + h]
            names = groups[:, block(source, size)].astype(f32)
            outs[buffer][rows : rows + 8, h * size : (h + 1) * size] = jnp.broadcast_to(
                names, (8, size)
            )


def split_field(field, wide, size):
    rows, width = field.shape
    high, low = high_low(field[...])
    wide[0:rows, 0:width] = high
    wide[rows : 2 * rows, 0:width] = low
    wide[:, width : width + size] = jnp.zeros((2 * rows, size), bf16)


def local_product(columns, matrix, wide, out, size):
    blocks, count = matrix.shape[0], matrix.shape[1]
    rows = out.shape[0]
    for g in range(blocks):
        parts = [wide[:, g * size : (g + 1) * size]]
        for k in range(1, count):
            column = jnp.minimum(columns[g * count + k], blocks)
            parts.append(wide[:, block(column, size)])
        product = dot_nt(
            jnp.concatenate(parts, axis=1),
            jnp.concatenate([matrix[g, k] for k in range(count)], axis=1),
        )
        out[:, g * size : (g + 1) * size] = product[:rows] + product[rows:]


def local_kernel(columns, field, matrix, out, wide, *, size):
    split_field(field, wide, size)
    local_product(columns, matrix, wide, out, size)


def prepare_kernel(
    meta, columns, field, matrix, groups, coarse, out, entries, inverse, onehot, coarse_high, coarse_low, coarse_inverse, wide, *, size, halo_slots
):
    blocks, count = matrix.shape[0], matrix.shape[1]
    limit = entries.shape[0] - 1

    def clear(i, carry):
        entries[i] = halo_slots
        return carry

    lax.fori_loop(0, limit, clear, 0)
    per = halo_slots // 4

    def scan(g, found):
        for k in range(1, count):
            column = columns[g * count + k]
            slot = jnp.maximum(column - blocks, 0)
            direction = lax.div(slot, per)
            flip = jnp.where(direction < 2, meta[0], meta[1])
            place = (direction ^ flip) * per + lax.rem(slot, per)
            use = jnp.where(column >= blocks, meta[2 + direction], 0)
            entries[found] = jnp.where(
                use > 0, (g * count + k) * (2 * halo_slots) + place, halo_slots
            )
            found = found + use
        return found

    total = lax.fori_loop(0, blocks, scan, 0)
    entries[limit] = total
    same = (
        lax.broadcasted_iota(jnp.int32, (size, size), 0)
        == lax.broadcasted_iota(jnp.int32, (size, size), 1)
    )
    for g in range(blocks):
        diagonal = jnp.sum(
            jnp.where(same, matrix[g, 0].astype(f32), 0.0), axis=0, keepdims=True
        )
        inverse[:, g * size : (g + 1) * size] = jnp.broadcast_to(1.0 / diagonal, (8, size))
    diagonal = jnp.sum(jnp.where(same, coarse[0], 0.0), axis=0, keepdims=True)
    coarse_inverse[...] = jnp.broadcast_to(1.0 / diagonal, (8, size))
    cells = lax.broadcasted_iota(jnp.int32, (size, groups.shape[1]), 0)
    onehot[...] = jnp.where(cells == groups[...], 1.0, 0.0).astype(bf16)
    for k in range(5):
        if k == 0:
            piece = coarse[0]
        else:
            direction = direction_of(meta, k - 1)
            piece = jnp.where(meta[2 + direction] > 0, coarse[1 + direction], 0.0)
        high, low = high_low(piece)
        coarse_high[:, k * size : (k + 1) * size] = high
        coarse_low[:, k * size : (k + 1) * size] = low
    split_field(field, wide, size)
    local_product(columns, matrix, wide, out, size)


def split_halos(halos, wide, size):
    rows = wide.shape[0] // 2
    width = halos[0].shape[1]
    for buffer in range(4):
        high, low = high_low(halos[buffer][0:rows, :])
        wide[0:rows, buffer * width : (buffer + 1) * width] = high
        wide[rows : 2 * rows, buffer * width : (buffer + 1) * width] = low
    wide[:, 4 * width : 4 * width + size] = jnp.zeros((2 * rows, size), bf16)


def subtract_halo(entries, matrix, wide, products, residual, size):
    blocks, count = matrix.shape[0], matrix.shape[1]
    rows = residual.shape[0]
    slots = wide.shape[1] // size - 1
    limit = entries.shape[0] - 1

    def chunk(c, carry):
        for i in range(CHUNK):
            code = entries[c * CHUNK + i]
            which, place = lax.div(code, 2 * slots), lax.rem(code, 2 * slots)
            product = dot_nt(
                wide[:, block(place, size)], matrix[lax.div(which, count), lax.rem(which, count)]
            )
            products[i] = product[:rows] + product[rows:]
        for i in range(CHUNK):
            row = lax.div(entries[c * CHUNK + i], 2 * slots * count)
            at = block(row, size)
            residual[:, at] = residual[:, at] - products[i]
        return carry

    lax.fori_loop(0, (entries[limit] + CHUNK - 1) // CHUNK, chunk, 0)


def halo_kernel(
    *refs, size, weights, first, mode
):
    refs = list(refs)
    meta, lists, entries = refs[:3]
    halos = refs[3:7]
    local, residual, update, iterate, inverse, matrix = refs[7:13]
    refs = refs[13:]
    rows = local.shape[0]
    if mode == "restrict":
        onehot, coarse_inverse, left_out, start_out, coarse_out, wide, products = refs
        residual_out = left_out
    elif mode == "last":
        iterate_out, residual_out, wide, products = refs
    else:
        residual_out, update_out, iterate_out = refs[:3]
        outs = refs[3:7]
        wide, products = refs[7:]
    split_halos(halos, wide, size)
    residual_out[...] = residual[...] - local[...]
    subtract_halo(entries, matrix, wide, products, residual_out, size)
    if mode == "restrict":
        high, low = high_low(residual_out[...])
        total = dot_nt(jnp.concatenate([high, low], axis=0), onehot[...])
        total = total[:rows] + total[rows:]
        coarse_out[...] = total
        start_out[...] = coarse_inverse[0:1, :] * total / center_value
        return
    if first:
        new = inverse[0:1, :] * residual_out[...] / center_value
    else:
        new = weights[0] * update[...] + weights[1] * inverse[0:1, :] * residual_out[...]
    iterate_out[...] = iterate[...] + new
    if mode == "send":
        update_out[...] = new
        pack(meta, lists, update_out, outs, size)


def coarse_product(c, halos, coarse_high, coarse_low):
    rows = c.shape[0]
    high, low = high_low(jnp.concatenate([c] + [h[...] for h in halos], axis=1))
    big = dot_nt(jnp.concatenate([high, low], axis=0), coarse_high[...])
    return big[:rows] + big[rows:] + dot_nt(high, coarse_low[...])


def coarse_kernel(
    h0, h1, h2, h3, residual, update, iterate, coarse_high, coarse_low, coarse_inverse, *outs, weights, last
):
    c = update[...]
    left = residual[...] - coarse_product(c, (h0, h1, h2, h3), coarse_high, coarse_low)
    new = weights[0] * c + weights[1] * coarse_inverse[0:1, :] * left
    if last:
        outs[0][...] = iterate[...] + new
    else:
        residual_out, update_out, iterate_out = outs
        residual_out[...] = left
        update_out[...] = new
        iterate_out[...] = iterate[...] + new


def spread_kernel(columns, correction, onehot, iterate, matrix, second, out, field, wide, *, size):
    rows = correction.shape[0]
    high, low = high_low(correction[...])
    spread = dot_nn(jnp.concatenate([high, low], axis=0), onehot[...])
    field[...] = spread[:rows] + spread[rows:]
    second[...] = iterate[...] + field[...]
    split_field(field, wide, size)
    local_product(columns, matrix, wide, out, size)


def names_kernel(n0, n1, n2, n3, out, *, size):
    width = n0.shape[1]
    for buffer, names in enumerate((n0, n1, n2, n3)):
        cells = lax.broadcasted_iota(jnp.int32, (size, width), 0).astype(f32)
        out[:, buffer * width : (buffer + 1) * width] = jnp.where(
            cells == names[0:1, :], 1.0, 0.0
        ).astype(bf16)


def second_kernel(
    meta, lists, entries, e0, e1, e2, e3, names, local, leftover, iterate, inverse, matrix, residual_out, update_out, iterate_out, o0, o1, o2, o3, wide, products, *, size
):
    rows = local.shape[0]
    width = names.shape[1] // 4
    for buffer, e in enumerate((e0, e1, e2, e3)):
        high, low = high_low(e[...])
        spread = dot_nn(
            jnp.concatenate([high, low], axis=0),
            names[:, buffer * width : (buffer + 1) * width],
        )
        high, low = high_low(spread[:rows] + spread[rows:])
        wide[0:rows, buffer * width : (buffer + 1) * width] = high
        wide[rows : 2 * rows, buffer * width : (buffer + 1) * width] = low
    wide[:, 4 * width : 4 * width + size] = jnp.zeros((2 * rows, size), bf16)
    residual_out[...] = leftover[...] - local[...]
    subtract_halo(entries, matrix, wide, products, residual_out, size)
    new = inverse[0:1, :] * residual_out[...] / center_value
    iterate_out[...] = iterate[...] + new
    update_out[...] = new
    pack(meta, lists, update_out, (o0, o1, o2, o3), size)


def local_program(
    right_side, start_guess, fine_matrix, fine_columns, send_lists, aggregates, coarse_matrix
):
    n_span, n_stream = lax.axis_size("span"), lax.axis_size("stream")
    rows, width = right_side.shape
    blocks, count, size, _ = fine_matrix.shape
    slots = send_lists.shape[1] // 4
    halo_width = slots * size
    perms = exchanges(n_span, n_stream)
    s, t = lax.axis_index("span"), lax.axis_index("stream")
    meta = jnp.stack(
        [
            1 - s % 2,
            1 - t % 2,
            (s > 0).astype(jnp.int32),
            (s < n_span - 1).astype(jnp.int32),
            (t > 0).astype(jnp.int32),
            (t < n_stream - 1).astype(jnp.int32),
        ]
    ).astype(jnp.int32)
    lists = send_lists.reshape(-1)
    columns = fine_columns.reshape(-1)
    groups = aggregates.reshape(1, width)
    coarse = coarse_matrix.reshape(coarse_matrix.shape[1:])
    weights = chebyshev_weights()

    vmem = pl.BlockSpec(memory_space=pltpu.VMEM)
    smem = pl.BlockSpec(memory_space=pltpu.SMEM)

    def call(kernel, ins, outs, scratch=(), scalars=0, scalar_outs=(), flops=0):
        return pl.pallas_call(
            kernel,
            out_shape=[jax.ShapeDtypeStruct(shape, kind) for shape, kind in outs],
            in_specs=[smem] * scalars + [vmem] * (len(ins) - scalars),
            out_specs=[smem if i in scalar_outs else vmem for i in range(len(outs))],
            scratch_shapes=list(scratch),
            compiler_params=pltpu.CompilerParams(vmem_limit_bytes=VMEM_LIMIT),
            cost_estimate=pl.CostEstimate(
                flops=flops, bytes_accessed=4 * 1024 * 1024, transcendentals=0
            ),
        )(*ins)

    def exchange(payloads):
        return [lax.ppermute(x, AXES, perm) for x, perm in zip(payloads, perms)]

    field = ((rows, width), f32)
    halo = ((rows, halo_width), f32)
    small = ((rows, size), f32)
    wide_local = pltpu.VMEM((2 * rows, width + size), bf16)
    wide_halo = pltpu.VMEM((2 * rows, 4 * halo_width + size), bf16)
    products = pltpu.VMEM((CHUNK, rows, size), f32)
    flops = 2 * 2 * rows * blocks * count * size * size

    def apply_local(update):
        return call(
            functools.partial(local_kernel, size=size),
            [columns, update, fine_matrix], [field], [wide_local], 1, flops=flops,
        )[0]

    def sweep(halos, local, residual, update, iterate, weight, first=False, mode="send", extra=()):
        outs = {
            "send": [field, field, field] + [halo] * 4,
            "last": [field, field],
            "restrict": [field, small, small],
        }[mode]
        return call(
            functools.partial(halo_kernel, size=size, weights=weight, first=first, mode=mode),
            [meta, lists, entries] + halos + [local, residual, update, iterate, inverse, fine_matrix] + list(extra),
            outs, [wide_halo, products], 3, flops=flops // 5,
        )

    payloads = call(
        functools.partial(pack_kernel, size=size),
        [meta, lists, start_guess, groups], [((rows + 8, halo_width), f32)] * 4, (), 2,
    )
    entry_count = -(-blocks * (count - 1) // CHUNK) * CHUNK
    halos = exchange(payloads)
    local, entries, inverse, onehot, coarse_high, coarse_low, coarse_inverse = call(
        functools.partial(prepare_kernel, size=size, halo_slots=4 * slots),
        [meta, columns, start_guess, fine_matrix, groups, coarse],
        [
            field,
            ((entry_count + 1,), jnp.int32),
            ((8, width), f32),
            ((size, width), bf16),
            ((size, 5 * size), bf16),
            ((size, 5 * size), bf16),
            ((8, size), f32),
        ],
        [wide_local], 2, (1,), flops=flops,
    )
    names = [h[rows : rows + 8] for h in halos]
    residual, update, iterate, *payloads = sweep(
        halos, local, right_side, start_guess, start_guess, (0.0, 0.0), first=True
    )
    for weight in weights:
        halos = exchange(payloads)
        local = apply_local(update)
        residual, update, iterate, *payloads = sweep(
            halos, local, residual, update, iterate, weight
        )
    halos = exchange(payloads)
    local = apply_local(update)
    names = call(
        functools.partial(names_kernel, size=size), names, [((size, 4 * halo_width), bf16)]
    )[0]
    leftover, c, coarse_left = sweep(
        halos, local, residual, update, iterate, (0.0, 0.0), mode="restrict",
        extra=(onehot, coarse_inverse),
    )
    correction = c
    for i, weight in enumerate(weights):
        halos = exchange([c] * 4)
        result = call(
            functools.partial(coarse_kernel, weights=weight, last=i == 1),
            halos + [coarse_left, c, correction, coarse_high, coarse_low, coarse_inverse],
            [small] if i == 1 else [small] * 3,
        )
        if i == 1:
            correction = result[0]
        else:
            coarse_left, c, correction = result
    halos = exchange([correction] * 4)
    iterate, local = call(
        functools.partial(spread_kernel, size=size),
        [columns, correction, onehot, iterate, fine_matrix], [field, field],
        [pltpu.VMEM((rows, width), f32), wide_local], 1, flops=flops,
    )
    residual, update, iterate, *payloads = call(
        functools.partial(second_kernel, size=size),
        [meta, lists, entries] + halos + [names, local, leftover, iterate, inverse, fine_matrix],
        [field, field, field] + [halo] * 4, [wide_halo, products], 3, flops=flops // 5,
    )
    halos = exchange(payloads)
    local = apply_local(update)
    residual, update, iterate, *payloads = sweep(
        halos, local, residual, update, iterate, weights[0]
    )
    halos = exchange(payloads)
    local = apply_local(update)
    result = sweep(halos, local, residual, update, iterate, weights[1], mode="last")
    return (result[0], correction)


VMEM_LIMIT = 16 * 1024 * 1024


def solution(mesh):
    placed = (
        P(None, AXES),
        P(None, AXES),
        P(AXES, None, None, None),
        P(AXES, None),
        P(AXES, None),
        P(AXES),
        P(AXES, None, None, None),
    )
    return jax.shard_map(
        local_program,
        mesh=mesh,
        in_specs=placed,
        out_specs=(P(None, AXES), P(None, AXES)),
        check_vma=False,
    )
```

```python
import functools

import jax
import jax.numpy as jnp
from jax import lax
from jax.experimental import pallas as pl
from jax.experimental.pallas import tpu as pltpu
from jax.sharding import PartitionSpec as P

center_value = 1.1
radius_value = 0.9
AXES = ("span", "stream")
ORDER = (2, 0, 1, 3)
EARLY = (0, 1, 2)
LAST = 3
CHUNK = 4
VMEM_LIMIT = 16 * 1024 * 1024
f32 = jnp.float32
bf16 = jnp.bfloat16
i32 = jnp.int32


def chebyshev_weights():
    weights = []
    old = radius_value / center_value
    for _ in range(2):
        now = 1.0 / (2.0 * center_value / radius_value - old)
        weights.append((now * old, 2.0 * now / radius_value))
        old = now
    return weights


def even_partner(i, n):
    return i ^ 1 if (i ^ 1) < n else None


def odd_partner(i, n):
    j = ((i + 1) ^ 1) - 1
    return j if 0 <= j < n else None


def exchanges(n_span, n_stream):
    def flat(rule):
        return [(s * n_stream + t, rule(s, t)) for s in range(n_span) for t in range(n_stream)]

    def along_span(rule):
        def pick(s, t):
            other = rule(s, n_span)
            if other is not None:
                return other * n_stream + t
            spare = even_partner(t, n_stream)
            return s * n_stream + (t if spare is None else spare)

        return pick

    def along_stream(rule):
        def pick(s, t):
            other = rule(t, n_stream)
            if other is not None:
                return s * n_stream + other
            spare = even_partner(s, n_span)
            return (s if spare is None else spare) * n_stream + t

        return pick

    return [
        flat(along_span(even_partner)),
        flat(along_span(odd_partner)),
        flat(along_stream(even_partner)),
        flat(along_stream(odd_partner)),
    ]


def place_in_mesh():
    s, t = lax.axis_index("span"), lax.axis_index("stream")
    n_span, n_stream = lax.axis_size("span"), lax.axis_size("stream")
    flips = (1 - (s & 1), 1 - (t & 1))
    valid = tuple(
        jnp.where(there, 1, 0).astype(i32)
        for there in (s > 0, s < n_span - 1, t > 0, t < n_stream - 1)
    )
    return flips, valid


def dot_nt(a, b):
    return lax.dot_general(a, b, (((1,), (1,)), ((), ())), preferred_element_type=f32)


def dot_nn(a, b):
    return lax.dot_general(a, b, (((1,), (0,)), ((), ())), preferred_element_type=f32)


def high_low(x):
    high = x.astype(bf16)
    return high, (x - high.astype(f32)).astype(bf16)


def stacked(x):
    return jnp.concatenate(high_low(x), axis=0)


def halves(x):
    rows = x.shape[0] // 2
    return x[:rows] + x[rows:]


def block(index, size):
    return pl.ds(pl.multiple_of(index * size, size), size)


class Table:
    def __init__(self, blocks, count, slots):
        self.blocks, self.count, self.slots = blocks, count, slots
        self.capacity = blocks * (count - 1) + CHUNK
        self.columns = 4 * slots
        self.home = self.columns + blocks * count
        self.counts = self.home + 5
        self.entries = self.counts + 5
        self.length = self.entries + 5 * self.capacity

    def direction(self, slot):
        if self.slots & (self.slots - 1) == 0:
            return slot >> (self.slots.bit_length() - 1)
        return lax.div(slot, self.slots)

    def code(self, which, row, slot):
        return (which << 16) | (row << 8) | slot


def pack(table, field, outs, size, slots):
    for buffer in range(4):
        for h in range(slots):
            source = table[buffer * slots + h]
            outs[buffer][:, h * size : (h + 1) * size] = field[:, block(source, size)]


def load_kernel(
    guess, lists, columns, groups, o0, o1, o2, o3, field, lists_out, columns_out, names, sems, *, size, slots
):
    copies = [
        pltpu.make_async_copy(source, target, sems.at[i])
        for i, (source, target) in enumerate(
            ((lists, lists_out), (guess, field), (groups, names), (columns, columns_out))
        )
    ]
    for copy in copies:
        copy.start()
    flips, _ = place_in_mesh()
    for copy in copies:
        copy.wait()
    rows = field.shape[0]
    for buffer, out in enumerate((o0, o1, o2, o3)):
        direction = buffer ^ flips[buffer // 2]
        for h in range(slots):
            at = block(lists_out[0, direction * slots + h], size)
            out[0:rows, h * size : (h + 1) * size] = field[:, at]
            out[rows : rows + 8, h * size : (h + 1) * size] = jnp.broadcast_to(
                names[:, at].astype(f32), (8, size)
            )


def split_field(field, wide, size):
    rows, width = field.shape
    high, low = high_low(field[...])
    wide[0:rows, 0:width] = high
    wide[rows : 2 * rows, 0:width] = low
    wide[:, width : width + size] = jnp.zeros((2 * rows, size), bf16)


def local_block(table, lay, matrix, wide, g, size):
    parts = [wide[:, g * size : (g + 1) * size]]
    for k in range(1, lay.count):
        parts.append(wide[:, block(table[lay.columns + g * lay.count + k], size)])
    pieces = [matrix[g * lay.count + k] for k in range(lay.count)]
    return halves(dot_nt(jnp.concatenate(parts, axis=1), jnp.concatenate(pieces, axis=1)))


def diagonal_row(matrix, same):
    return jnp.sum(jnp.where(same, matrix.astype(f32), 0.0), axis=0, keepdims=True)


def square_mask(size):
    return lax.broadcasted_iota(i32, (size, size), 0) == lax.broadcasted_iota(
        i32, (size, size), 1
    )


def build_table(lists, columns, table, lay):
    flips, valid = place_in_mesh()
    for direction in range(4):
        buffer = direction ^ flips[direction // 2]
        table[lay.home + direction] = jnp.where(valid[direction] > 0, buffer, 4)
        for h in range(lay.slots):
            table[buffer * lay.slots + h] = lists[0, direction * lay.slots + h]
    table[lay.home + 4] = 4
    for buffer in range(5):
        table[lay.counts + buffer] = 0
    for g in range(lay.blocks):
        table[lay.columns + g * lay.count] = columns[0, g]
        for k in range(1, lay.count):
            column = columns[k, g]
            table[lay.columns + g * lay.count + k] = jnp.minimum(column, lay.blocks)
            slot = jnp.maximum(column - lay.blocks, 0)
            direction = jnp.where(column < lay.blocks, 4, lay.direction(slot))
            buffer = table[lay.home + direction]
            found = table[lay.counts + buffer]
            table[lay.entries + buffer * lay.capacity + found] = lay.code(
                g * lay.count + k, g, slot - lay.direction(slot) * lay.slots
            )
            table[lay.counts + buffer] = found + 1
    for buffer in range(4):
        found = table[lay.counts + buffer]
        for i in range(CHUNK):
            table[lay.entries + buffer * lay.capacity + found + i] = lay.slots


def first_kernel(
    lists, columns, field, target, source, out, table, inverse, matrix, wide, right, sems, *, size, lay, parts
):
    per = matrix.shape[0] // parts
    copies = [
        pltpu.make_async_copy(
            source.at[pl.ds(i * per, per)], matrix.at[pl.ds(i * per, per)], sems.at[i]
        )
        for i in range(parts)
    ]
    copies.append(pltpu.make_async_copy(target, right, sems.at[parts]))
    for copy in copies:
        copy.start()
    split_field(field, wide, size)
    build_table(lists, columns, table, lay)
    copies[parts].wait()
    same = square_mask(size)
    for g in range(lay.blocks):
        if g % (lay.blocks // parts) == 0:
            copies[g // (lay.blocks // parts)].wait()
        at = slice(g * size, (g + 1) * size)
        out[:, at] = right[:, at] - local_block(table, lay, matrix, wide, g, size)
        inverse[:, at] = jnp.broadcast_to(
            1.0 / diagonal_row(matrix[g * lay.count], same), (8, size)
        )


def local_kernel(table, update, residual, iterate, matrix, out, iterate_out, wide, *, size, lay):
    split_field(update, wide, size)
    for g in range(lay.blocks):
        at = slice(g * size, (g + 1) * size)
        out[:, at] = residual[:, at] - local_block(table, lay, matrix, wide, g, size)
    iterate_out[...] = iterate[...] + update[...]


def local_and_coarse_kernel(
    table, update, residual, iterate, matrix, groups, coarse, h0, h1, h2, h3,
    out, iterate_out, onehot, names, coarse_high, coarse_low, coarse_inverse, wide, brought, cells, sems, *, size, lay,
):
    copies = [
        pltpu.make_async_copy(coarse, brought, sems.at[0]),
        pltpu.make_async_copy(groups, cells, sems.at[1]),
    ]
    for copy in copies:
        copy.start()
    local_kernel(
        table, update, residual, iterate, matrix, out, iterate_out, wide, size=size, lay=lay
    )
    width = lay.slots * size
    rows = update.shape[0]
    number = lax.broadcasted_iota(i32, (size, width), 0).astype(f32)
    for buffer, received in enumerate((h0, h1, h2, h3)):
        names[:, buffer * width : (buffer + 1) * width] = jnp.where(
            number == received[rows : rows + 1, :], 1.0, 0.0
        ).astype(bf16)
    for copy in copies:
        copy.wait()
    onehot[...] = jnp.where(
        lax.broadcasted_iota(i32, onehot.shape, 0) == cells[...], 1.0, 0.0
    ).astype(bf16)
    coarse_inverse[...] = jnp.broadcast_to(
        1.0 / diagonal_row(brought[0], square_mask(size)), (8, size)
    )
    flips, valid = place_in_mesh()
    for k in range(5):
        if k == 0:
            piece = brought[0]
        else:
            direction = (k - 1) ^ flips[(k - 1) // 2]
            there = jnp.where(
                direction < 2,
                jnp.where(direction == 0, valid[0], valid[1]),
                jnp.where(direction == 2, valid[2], valid[3]),
            )
            piece = jnp.where(there > 0, brought[1 + direction], 0.0)
        high, low = high_low(piece)
        coarse_high[:, k * size : (k + 1) * size] = high
        coarse_low[:, k * size : (k + 1) * size] = low


def put_halo(wide, place, x, size):
    rows, width = x.shape
    start = place * (width + size)
    high, low = high_low(x)
    wide[0:rows, start : start + width] = high
    wide[rows : 2 * rows, start : start + width] = low
    wide[:, start + width : start + width + size] = jnp.zeros((2 * rows, size), bf16)


def entry_product(code, matrix, wide, place, lay, size):
    which, row, slot = code >> 16, (code >> 8) & 255, code & 255
    at = block(place * (lay.slots + 1) + slot, size)
    return block(row, size), halves(dot_nt(wide[:, at], matrix[which]))


def for_received(table, lay, buffers, matrix, wide, size, use):
    def group(members):
        use(
            [
                entry_product(
                    table[lay.entries + buffer * lay.capacity + i], matrix, wide, place, lay, size
                )
                for place, buffer, i in members
            ]
        )

    group([(p, b, i) for p, b in enumerate(buffers) for i in range(CHUNK)])
    for place, buffer in enumerate(buffers):

        def more(c, carry, place=place, buffer=buffer):
            group([(place, buffer, c * CHUNK + i) for i in range(CHUNK)])
            return carry

        chunks = (table[lay.counts + buffer] + CHUNK - 1) // CHUNK
        lax.fori_loop(1, chunks, more, 0)


def sweep_weights(weights, inverse):
    if weights is None:
        return None, inverse[0:1, :] / center_value
    return weights[0], weights[1] * inverse[0:1, :]


def early_kernel(table, h0, h1, h2, residual, update, inverse, matrix, *refs, size, lay, weights, mode):
    refs = list(refs)
    rows = residual.shape[0]
    onehot = refs.pop(0) if mode == "restrict" else None
    names = refs.pop(0) if mode == "spread" else None
    iterate = refs.pop(0) if mode == "last" else None
    left, new, wide = refs
    for place, received in enumerate((h0, h1, h2)):
        if mode == "spread":
            width = lay.slots * size
            buffer = EARLY[place]
            chosen = names[:, buffer * width : (buffer + 1) * width]
            put_halo(wide, place, halves(dot_nn(stacked(received[...]), chosen)), size)
        else:
            put_halo(wide, place, received[0:rows, :], size)
    left[...] = residual[...]

    def use(found):
        for at, product in found:
            left[:, at] = left[:, at] - product

    for_received(table, lay, EARLY, matrix, wide, size, use)
    if mode == "restrict":
        new[...] = halves(dot_nt(stacked(left[...]), onehot[...]))
        return
    a, b = sweep_weights(weights, inverse)
    change = b * left[...] if a is None else a * update[...] + b * left[...]
    new[...] = iterate[...] + change if mode == "last" else change


def late_kernel(table, received, residual, update, inverse, matrix, *refs, size, lay, weights, mode):
    refs = list(refs)
    rows = residual.shape[0]
    names = refs.pop(0) if mode == "spread" else None
    wide, scaled = refs[-2:]
    if mode == "last":
        new = refs[0]
        new[...] = update[...]
    else:
        left, new = refs[:2]
    if mode == "spread":
        width = lay.slots * size
        chosen = names[:, LAST * width : (LAST + 1) * width]
        put_halo(wide, 0, halves(dot_nn(stacked(received[...]), chosen)), size)
    else:
        put_halo(wide, 0, received[0:rows, :], size)
    scaled[0:1, :] = sweep_weights(weights, inverse)[1]

    def use(found):
        for at, product in found:
            if mode != "last":
                left[:, at] = left[:, at] - product
            new[:, at] = new[:, at] - scaled[0:1, at] * product

    for_received(table, lay, (LAST,), matrix, wide, size, use)
    if mode != "last":
        pack(table, new, refs[2:6], size, lay.slots)


def restrict_kernel(
    table, received, residual, matrix, onehot, part, coarse_inverse, left, total, start, wide, *, size, lay
):
    rows = residual.shape[0]
    put_halo(wide, 0, received[0:rows, :], size)
    total[...] = part[...]

    def use(found):
        for at, product in found:
            left[:, at] = left[:, at] - product
        amount = sum(halves(dot_nt(stacked(product), onehot[:, at])) for at, product in found)
        total[...] = total[...] - amount

    for_received(table, lay, (LAST,), matrix, wide, size, use)
    start[...] = coarse_inverse[0:1, :] * total[...] / center_value


def coarse_kernel(
    h0, h1, h2, h3, residual, update, iterate, coarse_high, coarse_low, coarse_inverse, *outs, weights, last
):
    c = update[...]
    rows = c.shape[0]
    high, low = high_low(jnp.concatenate([c] + [h[...] for h in (h0, h1, h2, h3)], axis=1))
    product = halves(dot_nt(jnp.concatenate([high, low], axis=0), coarse_high[...]))
    left = residual[...] - (product + dot_nt(high, coarse_low[...]))
    new = weights[0] * c + weights[1] * coarse_inverse[0:1, :] * left
    outs[0][...] = iterate[...] + new
    if not last:
        outs[1][...] = left
        outs[2][...] = new


def spread_kernel(
    table, correction, onehot, iterate, leftover, matrix, second, out, correction_out, field, wide, *, size, lay
):
    field[...] = halves(dot_nn(stacked(correction[...]), onehot[...]))
    local_kernel(table, field, leftover, iterate, matrix, out, second, wide, size=size, lay=lay)
    correction_out[...] = correction[...]


def local_program(
    right_side, start_guess, fine_matrix, fine_columns, send_lists, aggregates, coarse_matrix
):
    perms = exchanges(lax.axis_size("span"), lax.axis_size("stream"))
    rows, width = right_side.shape
    blocks, count, size, _ = fine_matrix.shape
    slots = send_lists.shape[1] // 4
    halo_width = slots * size
    lay = Table(blocks, count, slots)
    groups = aggregates.reshape(1, width)
    stored = fine_matrix.reshape(blocks * count, size, size)
    coarse = coarse_matrix.reshape(coarse_matrix.shape[1:])
    weights = chebyshev_weights()
    parts = 4 if blocks % 4 == 0 else 1

    spaces = {
        "v": pl.BlockSpec(memory_space=pltpu.VMEM),
        "s": pl.BlockSpec(memory_space=pltpu.SMEM),
        "h": pl.BlockSpec(memory_space=pltpu.HBM),
    }

    def call(kernel, ins, outs, scratch=(), where="", kept="", aliases=None, flops=0, **named):
        where = where + "v" * (len(ins) - len(where))
        kept = kept + "v" * (len(outs) - len(kept))
        fixed = {"h": pltpu.HBM, "V": pltpu.VMEM}
        ins = [
            pltpu.with_memory_space_constraint(x, fixed[c]) if c in fixed else x
            for x, c in zip(ins, where)
        ]
        forms = {
            "v": jax.ShapeDtypeStruct,
            "V": pltpu.MemorySpace.VMEM,
            "s": pltpu.MemorySpace.SMEM,
        }
        return pl.pallas_call(
            functools.partial(kernel, **named),
            out_shape=[forms[c](shape, kind) for c, (shape, kind) in zip(kept, outs)],
            in_specs=[spaces[c.lower()] for c in where],
            out_specs=[spaces[c.lower()] for c in kept],
            scratch_shapes=list(scratch),
            input_output_aliases=aliases or {},
            compiler_params=pltpu.CompilerParams(vmem_limit_bytes=VMEM_LIMIT),
            cost_estimate=pl.CostEstimate(
                flops=flops, bytes_accessed=4 * 1024 * 1024, transcendentals=0
            ),
        )(*ins)

    def exchange(payloads):
        got = [None] * 4
        for buffer in ORDER:
            got[buffer] = lax.ppermute(payloads[buffer], AXES, perms[buffer])
        return got

    field = ((rows, width), f32)
    halo = ((rows, halo_width), f32)
    small = ((rows, size), f32)
    wide_local = pltpu.VMEM((2 * rows, width + size), bf16)
    wide_early = pltpu.VMEM((2 * rows, 3 * (halo_width + size)), bf16)
    wide_late = pltpu.VMEM((2 * rows, halo_width + size), bf16)
    flops = 2 * 2 * rows * blocks * count * size * size
    dims = {"size": size, "lay": lay}

    def early(halos, residual, update, weight, mode="plain", extra=()):
        return call(
            early_kernel,
            [table] + [halos[b] for b in EARLY] + [residual, update, inverse, matrix] + list(extra),
            [field, small if mode == "restrict" else field], [wide_early], "s",
            "vv" if mode == "last" else "Vv" if mode == "restrict" else "VV",
            flops=flops // 5, weights=weight, mode=mode, **dims,
        )

    def sweep(halos, residual, update, weight, mode="plain", extra=(), late_extra=()):
        residual, update = early(halos, residual, update, weight, mode, extra)
        ins = [table, halos[LAST], residual, update, inverse, matrix] + list(late_extra)
        scratch = [wide_late, pltpu.VMEM((8, width), f32)]
        named = dict(flops=flops // 10, weights=weight, mode=mode, **dims)
        if mode == "last":
            return call(late_kernel, ins, [field], scratch, "s", **named)
        return call(
            late_kernel, ins, [field, field] + [halo] * 4, scratch, "svVV", "VV",
            {2: 0, 3: 1}, **named,
        )

    def local(update, residual, iterate):
        return call(
            local_kernel, [table, update, residual, iterate, matrix], [field, field],
            [wide_local], "s", flops=flops, **dims,
        )

    *payloads, guess, lists, columns = call(
        load_kernel,
        [start_guess, send_lists, fine_columns.T, groups],
        [((rows + 8, halo_width), f32)] * 4
        + [field, (send_lists.shape, i32), (fine_columns.shape[::-1], i32)],
        [pltpu.VMEM((1, width), i32), pltpu.SemaphoreType.DMA((4,))],
        "hhhh", "vvvvvss", size=size, slots=slots,
    )
    first_halos = halos = exchange(payloads)
    residual, table, inverse, matrix = call(
        first_kernel,
        [lists, columns, guess, right_side, stored],
        [field, ((lay.length,), i32), ((8, width), f32), (stored.shape, bf16)],
        [wide_local, pltpu.VMEM(*field), pltpu.SemaphoreType.DMA((parts + 1,))],
        "ssvhh", "vs", flops=flops, parts=parts, **dims,
    )
    iterate = guess
    residual, update, *payloads = sweep(halos, residual, guess, None)
    halos = exchange(payloads)
    residual, iterate, onehot, names, coarse_high, coarse_low, coarse_inverse = call(
        local_and_coarse_kernel,
        [table, update, residual, iterate, matrix, groups, coarse] + first_halos,
        [
            field,
            field,
            ((size, width), bf16),
            ((size, 4 * halo_width), bf16),
            ((size, 5 * size), bf16),
            ((size, 5 * size), bf16),
            ((8, size), f32),
        ],
        [
            wide_local,
            pltpu.VMEM(coarse.shape, f32),
            pltpu.VMEM((1, width), i32),
            pltpu.SemaphoreType.DMA((2,)),
        ],
        "svvvvhh", flops=flops, **dims,
    )
    residual, update, *payloads = sweep(halos, residual, update, weights[0])
    halos = exchange(payloads)
    residual, iterate = local(update, residual, iterate)
    residual, update, *payloads = sweep(halos, residual, update, weights[1])
    halos = exchange(payloads)
    residual, iterate = local(update, residual, iterate)
    residual, part = early(halos, residual, update, None, "restrict", (onehot,))
    leftover, coarse_left, c = call(
        restrict_kernel,
        [table, halos[LAST], residual, matrix, onehot, part, coarse_inverse],
        [field, small, small], [wide_late], "svV", "V", {2: 0}, flops=flops // 10, **dims,
    )
    correction = c
    for i, weight in enumerate(weights):
        halos = exchange([c] * 4)
        result = call(
            coarse_kernel,
            halos + [coarse_left, c, correction, coarse_high, coarse_low, coarse_inverse],
            [small] if i == 1 else [small] * 3, weights=weight, last=i == 1,
        )
        correction = result[0]
        if i == 0:
            coarse_left, c = result[1:]
    halos = exchange([correction] * 4)
    iterate, residual, correction_out = call(
        spread_kernel,
        [table, correction, onehot, iterate, leftover, matrix], [field, field, small],
        [pltpu.VMEM(*field), wide_local], "s", flops=flops, **dims,
    )
    residual, update, *payloads = sweep(
        halos, residual, iterate, None, "spread", (names,), (names,)
    )
    halos = exchange(payloads)
    residual, iterate = local(update, residual, iterate)
    residual, update, *payloads = sweep(halos, residual, update, weights[0])
    halos = exchange(payloads)
    residual, iterate = local(update, residual, iterate)
    result = sweep(halos, residual, update, weights[1], "last", (iterate,))
    return (result[0], correction_out)


def solution(mesh):
    placed = (
        P(None, AXES),
        P(None, AXES),
        P(AXES, None, None, None),
        P(AXES, None),
        P(AXES, None),
        P(AXES),
        P(AXES, None, None, None),
    )
    return jax.shard_map(
        local_program,
        mesh=mesh,
        in_specs=placed,
        out_specs=(P(None, AXES), P(None, AXES)),
        check_vma=False,
    )
```

```python
import functools

import jax
import jax.numpy as jnp
import numpy as np
from jax import lax
from jax.experimental import pallas as pl
from jax.experimental.pallas import tpu as pltpu
from jax.sharding import PartitionSpec as P

center_value = 1.1
radius_value = 0.9
AXES = ("span", "stream")
STEPS = ((0,), (1, 2, 3))
AHEAD = 2
COARSE = (3, 2, 1, 0)
CHUNK = 4
VMEM_LIMIT = 16 * 1024 * 1024
f32 = jnp.float32
bf16 = jnp.bfloat16
i32 = jnp.int32


def chebyshev_weights():
    weights = []
    old = radius_value / center_value
    for _ in range(2):
        now = 1.0 / (2.0 * center_value / radius_value - old)
        weights.append((now * old, 2.0 * now / radius_value))
        old = now
    return weights


def directions(s, t, n_span, n_stream, choose):
    span_even, span_odd = choose((s & 1) == 0, 1, 0), choose((s & 1) == 0, 0, 1)
    stream_even, stream_odd = choose((t & 1) == 0, 3, 2), choose((t & 1) == 0, 2, 3)
    end_s = (s == 0) | (s == n_span - 1)
    ahead = (((t + 1) >> 1) & 1) == 0
    return (
        choose(ahead, stream_odd, span_even),
        choose(ahead, span_even, choose(end_s, stream_odd, span_odd)),
        choose(ahead | end_s, span_odd, stream_odd),
        stream_even,
    )


def exchanges(n_span, n_stream):
    steps = ((-1, 0), (1, 0), (0, -1), (0, 1))
    partners = [{} for _ in range(4)]
    for s in range(n_span):
        for t in range(n_stream):
            way = directions(
                np.int32(s), np.int32(t), n_span, n_stream, lambda c, a, b: int(a if c else b)
            )
            for number in range(4):
                other_s, other_t = s + steps[way[number]][0], t + steps[way[number]][1]
                if 0 <= other_s < n_span and 0 <= other_t < n_stream:
                    partners[number][s, t] = (other_s, other_t)
    result = []
    for found in partners:
        idle = [(s, t) for s in range(n_span) for t in range(n_stream) if (s, t) not in found]
        while idle:
            s, t = idle.pop(0)
            other = min(
                idle,
                key=lambda o: (o != (s, t ^ 1), o[0] != s, abs(o[0] - s) + abs(o[1] - t)),
                default=(s, t),
            )
            if other in idle:
                idle.remove(other)
            found[s, t], found[other] = other, (s, t)
        result.append(
            [(s * n_stream + t, o[0] * n_stream + o[1]) for (s, t), o in sorted(found.items())]
        )
    return result


def place_in_mesh():
    s, t = lax.axis_index("span"), lax.axis_index("stream")
    n_span, n_stream = lax.axis_size("span"), lax.axis_size("stream")
    ways = directions(s, t, n_span, n_stream, jnp.where)
    there = [
        jnp.where(
            way < 2,
            jnp.where(way == 0, s > 0, s < n_span - 1),
            jnp.where(way == 2, t > 0, t < n_stream - 1),
        )
        for way in ways
    ]
    return ways, there


def dot_nt(a, b):
    return lax.dot_general(a, b, (((1,), (1,)), ((), ())), preferred_element_type=f32)


def dot_nn(a, b):
    return lax.dot_general(a, b, (((1,), (0,)), ((), ())), preferred_element_type=f32)


def high_low(x):
    high = x.astype(bf16)
    return high, (x - high.astype(f32)).astype(bf16)


def stacked(x):
    return jnp.concatenate(high_low(x), axis=0)


def halves(x):
    rows = x.shape[0] // 2
    return x[:rows] + x[rows:]


def block(index, size):
    return pl.ds(pl.multiple_of(index * size, size), size)


class Table:
    def __init__(self, blocks, count, slots):
        self.blocks, self.count, self.slots = blocks, count, slots
        self.capacity = blocks * (count - 1) + CHUNK
        self.columns = 4 * slots
        self.home = self.columns + blocks * count
        self.counts = self.home + 5
        self.entries = self.counts + 5
        self.length = self.entries + 5 * self.capacity

    def direction(self, slot):
        if self.slots & (self.slots - 1) == 0:
            return slot >> (self.slots.bit_length() - 1)
        return lax.div(slot, self.slots)

    def code(self, which, row, slot):
        return (which << 16) | (row << 8) | slot


def pack(table, field, outs, size, slots):
    for buffer in range(4):
        for h in range(slots):
            source = table[buffer * slots + h]
            outs[buffer][:, h * size : (h + 1) * size] = field[:, block(source, size)]


def load_kernel(
    guess, lists, columns, groups, o0, o1, o2, o3, field, lists_out, columns_out, names, sems, *, size, slots
):
    copies = [
        pltpu.make_async_copy(source, target, sems.at[i])
        for i, (source, target) in enumerate(
            ((lists, lists_out), (guess, field), (groups, names), (columns, columns_out))
        )
    ]
    for copy in copies:
        copy.start()
    ways, _ = place_in_mesh()
    for copy in copies:
        copy.wait()
    rows = field.shape[0]
    for buffer, out in enumerate((o0, o1, o2, o3)):
        direction = ways[buffer]
        for h in range(slots):
            at = block(lists_out[0, direction * slots + h], size)
            out[0:rows, h * size : (h + 1) * size] = field[:, at]
            out[rows : rows + 8, h * size : (h + 1) * size] = jnp.broadcast_to(
                names[:, at].astype(f32), (8, size)
            )


def split_field(field, wide, size):
    rows, width = field.shape
    high, low = high_low(field[...])
    wide[0:rows, 0:width] = high
    wide[rows : 2 * rows, 0:width] = low
    wide[0 : 2 * rows, width : width + size] = jnp.zeros((2 * rows, size), bf16)


def local_rows(table, lay, matrix, wide, g, size, rows):
    parts = [wide[0:rows, g * size : (g + 1) * size]]
    for k in range(1, lay.count):
        parts.append(wide[0:rows, block(table[lay.columns + g * lay.count + k], size)])
    pieces = [matrix[g * lay.count + k] for k in range(lay.count)]
    return dot_nt(jnp.concatenate(parts, axis=1), jnp.concatenate(pieces, axis=1))


def local_block(table, lay, matrix, wide, g, size, rows):
    return halves(local_rows(table, lay, matrix, wide, g, size, 2 * rows))


def diagonal_row(matrix, same):
    return jnp.sum(jnp.where(same, matrix.astype(f32), 0.0), axis=0, keepdims=True)


def square_mask(size):
    return lax.broadcasted_iota(i32, (size, size), 0) == lax.broadcasted_iota(
        i32, (size, size), 1
    )


def build_table(lists, columns, table, lay):
    ways, there = place_in_mesh()
    for buffer in range(4):
        direction = ways[buffer]
        table[lay.home + direction] = jnp.where(there[buffer], buffer, 4)
        for h in range(lay.slots):
            table[buffer * lay.slots + h] = lists[0, direction * lay.slots + h]
    table[lay.home + 4] = 4
    for buffer in range(5):
        table[lay.counts + buffer] = 0
    for g in range(lay.blocks):
        table[lay.columns + g * lay.count] = columns[0, g]
        for k in range(1, lay.count):
            column = columns[k, g]
            table[lay.columns + g * lay.count + k] = jnp.minimum(column, lay.blocks)
            slot = jnp.maximum(column - lay.blocks, 0)
            direction = jnp.where(column < lay.blocks, 4, lay.direction(slot))
            buffer = table[lay.home + direction]
            found = table[lay.counts + buffer]
            table[lay.entries + buffer * lay.capacity + found] = lay.code(
                g * lay.count + k, g, slot - lay.direction(slot) * lay.slots
            )
            table[lay.counts + buffer] = found + 1
    for buffer in range(4):
        found = table[lay.counts + buffer]
        for i in range(CHUNK):
            table[lay.entries + buffer * lay.capacity + found + i] = lay.slots


def sweep_weights(weights, inverse):
    if weights is None:
        return None, inverse[0:1, :] / center_value
    return weights[0], weights[1] * inverse[0:1, :]


def begin_sweep(left, update, iterate, inverse, new, weights, mode, onehot=None):
    if mode == "restrict":
        new[...] = halves(dot_nt(stacked(left[...]), onehot[...]))
        return
    a, b = sweep_weights(weights, inverse)
    change = b * left[...] if a is None else a * update[...] + b * left[...]
    new[...] = iterate[...] + change if mode == "last" else change


def first_kernel(
    lists, columns, field, target, source, left, new, table, inverse, matrix, wide, right, sems, *, size, lay, parts
):
    per = matrix.shape[0] // parts
    copies = [
        pltpu.make_async_copy(
            source.at[pl.ds(i * per, per)], matrix.at[pl.ds(i * per, per)], sems.at[i]
        )
        for i in range(parts)
    ]
    copies.append(pltpu.make_async_copy(target, right, sems.at[parts]))
    copies[parts].start()
    for copy in copies[:AHEAD]:
        copy.start()
    split_field(field, wide, size)
    build_table(lists, columns, table, lay)
    copies[parts].wait()
    same = square_mask(size)
    for g in range(lay.blocks):
        if g % (lay.blocks // parts) == 0:
            part = g // (lay.blocks // parts)
            copies[part].wait()
            if part + AHEAD < parts:
                copies[part + AHEAD].start()
        at = slice(g * size, (g + 1) * size)
        left[:, at] = right[:, at] - local_block(table, lay, matrix, wide, g, size, left.shape[0])
        inverse[:, at] = jnp.broadcast_to(
            1.0 / diagonal_row(matrix[g * lay.count], same), (8, size)
        )
    begin_sweep(left, None, None, inverse, new, None, "plain")


def local_kernel(table, update, residual, iterate, inverse, matrix, *refs, size, lay, weights, mode):
    refs = list(refs)
    onehot = refs.pop(0) if mode == "restrict" else None
    left, new, iterate_out, wide = refs
    split_field(update, wide, size)
    for g in range(lay.blocks):
        at = slice(g * size, (g + 1) * size)
        left[:, at] = residual[:, at] - local_block(table, lay, matrix, wide, g, size, left.shape[0])
    iterate_out[...] = iterate[...] + update[...]
    begin_sweep(left, update, iterate_out, inverse, new, weights, mode, onehot)


def local_and_coarse_kernel(
    table, update, residual, iterate, inverse, matrix, groups, coarse, h0, h1, h2, h3,
    left, new, iterate_out, onehot, names, coarse_high, coarse_low, coarse_inverse, wide, brought, cells, sems, *, size, lay, weights,
):
    copies = [
        pltpu.make_async_copy(coarse, brought, sems.at[0]),
        pltpu.make_async_copy(groups, cells, sems.at[1]),
    ]
    for copy in copies:
        copy.start()
    local_kernel(
        table, update, residual, iterate, inverse, matrix, left, new, iterate_out, wide,
        size=size, lay=lay, weights=weights, mode="plain",
    )
    width = lay.slots * size
    rows = update.shape[0]
    number = lax.broadcasted_iota(i32, (size, width), 0).astype(f32)
    for buffer, received in enumerate((h0, h1, h2, h3)):
        names[:, buffer * width : (buffer + 1) * width] = jnp.where(
            number == received[rows : rows + 1, :], 1.0, 0.0
        ).astype(bf16)
    for copy in copies:
        copy.wait()
    onehot[...] = jnp.where(
        lax.broadcasted_iota(i32, onehot.shape, 0) == cells[...], 1.0, 0.0
    ).astype(bf16)
    coarse_inverse[...] = jnp.broadcast_to(
        1.0 / diagonal_row(brought[0], square_mask(size)), (8, size)
    )
    ways, there = place_in_mesh()
    for k in range(5):
        if k == 0:
            piece = brought[0]
        else:
            piece = jnp.where(there[k - 1], brought[1 + ways[k - 1]], 0.0)
        high, low = high_low(piece)
        coarse_high[:, k * size : (k + 1) * size] = high
        coarse_low[:, k * size : (k + 1) * size] = low


def put_halo(wide, place, x, size):
    rows, width = x.shape
    start = place * (width + size)
    high, low = high_low(x)
    wide[0:rows, start : start + width] = high
    wide[rows : 2 * rows, start : start + width] = low
    wide[:, start + width : start + width + size] = jnp.zeros((2 * rows, size), bf16)


def put_halos(wide, halos, buffers, names, rows, lay, size):
    for place, (buffer, received) in enumerate(zip(buffers, halos)):
        x = received[0:rows, :]
        if names is not None:
            width = lay.slots * size
            chosen = names[:, buffer * width : (buffer + 1) * width]
            x = halves(dot_nn(stacked(x), chosen))
        put_halo(wide, place, x, size)


def entry_product(code, matrix, wide, place, lay, size):
    which, row, slot = code >> 16, (code >> 8) & 255, code & 255
    at = block(place * (lay.slots + 1) + slot, size)
    return block(row, size), halves(dot_nt(wide[:, at], matrix[which]))


def for_received(table, lay, buffers, matrix, wide, size, use):
    def group(members):
        use(
            [
                entry_product(
                    table[lay.entries + buffer * lay.capacity + i], matrix, wide, place, lay, size
                )
                for place, buffer, i in members
            ]
        )

    group([(p, b, i) for p, b in enumerate(buffers) for i in range(CHUNK)])
    for place, buffer in enumerate(buffers):

        def more(c, carry, place=place, buffer=buffer):
            group([(place, buffer, c * CHUNK + i) for i in range(CHUNK)])
            return carry

        chunks = (table[lay.counts + buffer] + CHUNK - 1) // CHUNK
        lax.fori_loop(1, chunks, more, 0)


def received_kernel(table, left_in, new_in, inverse, matrix, *refs, size, lay, weights, mode, buffers, final):
    refs = list(refs)
    halos, refs = refs[: len(buffers)], refs[len(buffers) :]
    rows = left_in.shape[0]
    names = refs.pop(0) if mode == "spread" else None
    if mode == "restrict":
        onehot, coarse_inverse = refs[:2]
        refs = refs[2:]
    wide, scaled = refs[-2:]
    left, new = refs[:2]
    if mode == "last" and final:
        new = refs[0]
        new[...] = new_in[...]
    put_halos(wide, halos, buffers, names, rows, lay, size)
    if mode != "restrict":
        scaled[0:1, :] = sweep_weights(weights, inverse)[1]

    def use(found):
        for at, product in found:
            if mode != "last":
                left[:, at] = left[:, at] - product
            if mode != "restrict":
                new[:, at] = new[:, at] - scaled[0:1, at] * product
        if mode == "restrict":
            new[...] = new[...] - sum(
                halves(dot_nt(stacked(product), onehot[:, at])) for at, product in found
            )

    for_received(table, lay, buffers, matrix, wide, size, use)
    if not final or mode == "last":
        return
    if mode == "restrict":
        refs[2][...] = coarse_inverse[0:1, :] * new[...] / center_value
    else:
        pack(table, new, refs[2:6], size, lay.slots)


def coarse_kernel(
    h0, h1, h2, h3, residual, update, iterate, coarse_high, coarse_low, coarse_inverse, *outs, weights, last
):
    c = update[...]
    rows = c.shape[0]
    received = dict(zip(COARSE, (h0, h1, h2, h3)))
    high, low = high_low(jnp.concatenate([c] + [received[b][...] for b in range(4)], axis=1))
    product = halves(dot_nt(jnp.concatenate([high, low], axis=0), coarse_high[...]))
    left = residual[...] - (product + dot_nt(high, coarse_low[...]))
    new = weights[0] * c + weights[1] * coarse_inverse[0:1, :] * left
    outs[0][...] = iterate[...] + new
    if not last:
        outs[1][...] = left
        outs[2][...] = new


def local_and_spread_kernel(
    table, update, residual, iterate, inverse, matrix, onehot, left, new, iterate_out, high, low, wide, *, size, lay, weights
):
    local_kernel(
        table, update, residual, iterate, inverse, matrix, left, new, iterate_out, wide,
        size=size, lay=lay, weights=weights, mode="plain",
    )
    width = onehot.shape[1]
    wide[0:size, 0:width] = onehot[...]
    wide[0:size, width : width + size] = jnp.zeros((size, size), bf16)
    for g in range(lay.blocks):
        at = slice(g * size, (g + 1) * size)
        high[:, at], low[:, at] = high_low(
            local_rows(table, lay, matrix, wide, g, size, size)
        )


def spread_kernel(
    table, correction, onehot, iterate, leftover, inverse, spread_high, spread_low, left, new, second, correction_out, *, size, lay
):
    rows = correction.shape[0]
    both = stacked(correction[...])
    second[...] = iterate[...] + halves(dot_nn(both, onehot[...]))
    product = halves(dot_nn(both, spread_high[...])) + dot_nn(both[:rows], spread_low[...])
    left[...] = leftover[...] - product
    begin_sweep(left, None, None, inverse, new, None, "plain")
    correction_out[...] = correction[...]


def local_program(
    right_side, start_guess, fine_matrix, fine_columns, send_lists, aggregates, coarse_matrix
):
    perms = exchanges(lax.axis_size("span"), lax.axis_size("stream"))
    rows, width = right_side.shape
    blocks, count, size, _ = fine_matrix.shape
    slots = send_lists.shape[1] // 4
    halo_width = slots * size
    lay = Table(blocks, count, slots)
    groups = aggregates.reshape(1, width)
    stored = fine_matrix.reshape(blocks * count, size, size)
    coarse = coarse_matrix.reshape(coarse_matrix.shape[1:])
    weights = chebyshev_weights()
    parts = 4 if blocks % 4 == 0 else 1

    spaces = {
        "v": pl.BlockSpec(memory_space=pltpu.VMEM),
        "s": pl.BlockSpec(memory_space=pltpu.SMEM),
        "h": pl.BlockSpec(memory_space=pltpu.HBM),
    }

    def call(kernel, ins, outs, scratch=(), where="", kept="", aliases=None, flops=0, **named):
        where = where + "v" * (len(ins) - len(where))
        kept = kept + "v" * (len(outs) - len(kept))
        fixed = {"h": pltpu.HBM, "V": pltpu.VMEM}
        ins = [
            pltpu.with_memory_space_constraint(x, fixed[c]) if c in fixed else x
            for x, c in zip(ins, where)
        ]
        forms = {
            "v": jax.ShapeDtypeStruct,
            "V": pltpu.MemorySpace.VMEM,
            "s": pltpu.MemorySpace.SMEM,
        }
        return pl.pallas_call(
            functools.partial(kernel, **named),
            out_shape=[forms[c](shape, kind) for c, (shape, kind) in zip(kept, outs)],
            in_specs=[spaces[c.lower()] for c in where],
            out_specs=[spaces[c.lower()] for c in kept],
            scratch_shapes=list(scratch),
            input_output_aliases=aliases or {},
            compiler_params=pltpu.CompilerParams(vmem_limit_bytes=VMEM_LIMIT),
            cost_estimate=pl.CostEstimate(
                flops=flops, bytes_accessed=4 * 1024 * 1024, transcendentals=0
            ),
        )(*ins)

    def exchange(payloads):
        return [lax.ppermute(x, AXES, perm) for x, perm in zip(payloads, perms)]

    field = ((rows, width), f32)
    halo = ((rows, halo_width), f32)
    small = ((rows, size), f32)
    wide_local = pltpu.VMEM((2 * rows, width + size), bf16)
    wide_spread = pltpu.VMEM((max(2 * rows, size), width + size), bf16)
    flops = 2 * 2 * rows * blocks * count * size * size
    dims = {"size": size, "lay": lay}

    def received(halos, left, new, weight, mode="plain", extra=()):
        for step, buffers in enumerate(STEPS):
            final = step == len(STEPS) - 1
            outs, kept = [field, small if mode == "restrict" else field], "VV"
            aliases = {1: 0, 2: 1}
            if mode == "last" and final:
                outs, kept, aliases = [field], "v", None
            elif mode == "restrict" and final:
                outs.append(small)
            elif final:
                outs += [halo] * 4
            result = call(
                received_kernel,
                [table, left, new, inverse, matrix] + [halos[b] for b in buffers] + list(extra),
                outs,
                [
                    pltpu.VMEM((2 * rows, len(buffers) * (halo_width + size)), bf16),
                    pltpu.VMEM((8, width), f32),
                ],
                "sVV", kept, aliases, flops=flops * len(buffers) // 20,
                weights=weight, mode=mode, buffers=buffers, final=final, **dims,
            )
            left, new = result[0], result[1] if len(result) > 1 else None
        return result

    def local(update, residual, iterate, weight, mode="plain", extra=()):
        return call(
            local_kernel, [table, update, residual, iterate, inverse, matrix] + list(extra),
            [field, small if mode == "restrict" else field, field],
            [wide_local], "s", "VV", flops=flops, weights=weight, mode=mode, **dims,
        )

    *payloads, guess, lists, columns = call(
        load_kernel,
        [start_guess, send_lists, fine_columns.T, groups],
        [((rows + 8, halo_width), f32)] * 4
        + [field, (send_lists.shape, i32), (fine_columns.shape[::-1], i32)],
        [pltpu.VMEM((1, width), i32), pltpu.SemaphoreType.DMA((4,))],
        "hhhh", "vvvvvss", size=size, slots=slots,
    )
    first_halos = halos = exchange(payloads)
    left, new, table, inverse, matrix = call(
        first_kernel,
        [lists, columns, guess, right_side, stored],
        [field, field, ((lay.length,), i32), ((8, width), f32), (stored.shape, bf16)],
        [wide_local, pltpu.VMEM(*field), pltpu.SemaphoreType.DMA((parts + 1,))],
        "ssvhh", "VVs", flops=flops, parts=parts, **dims,
    )
    residual, update, *payloads = received(halos, left, new, None)
    halos = exchange(payloads)
    left, new, iterate, onehot, names, coarse_high, coarse_low, coarse_inverse = call(
        local_and_coarse_kernel,
        [table, update, residual, guess, inverse, matrix, groups, coarse] + first_halos,
        [
            field,
            field,
            field,
            ((size, width), bf16),
            ((size, 4 * halo_width), bf16),
            ((size, 5 * size), bf16),
            ((size, 5 * size), bf16),
            ((8, size), f32),
        ],
        [
            wide_local,
            pltpu.VMEM(coarse.shape, f32),
            pltpu.VMEM((1, width), i32),
            pltpu.SemaphoreType.DMA((2,)),
        ],
        "svvvvvhh", "VV", flops=flops, weights=weights[0], **dims,
    )
    residual, update, *payloads = received(halos, left, new, weights[0])
    halos = exchange(payloads)
    left, new, iterate, spread_high, spread_low = call(
        local_and_spread_kernel, [table, update, residual, iterate, inverse, matrix, onehot],
        [field, field, field, ((size, width), bf16), ((size, width), bf16)],
        [wide_spread], "s", "VV", flops=flops, weights=weights[1], **dims,
    )
    residual, update, *payloads = received(halos, left, new, weights[1])
    halos = exchange(payloads)
    left, new, iterate = local(update, residual, iterate, None, "restrict", (onehot,))
    leftover, coarse_left, c = received(
        halos, left, new, None, "restrict", (onehot, coarse_inverse)
    )
    correction = c
    for i, weight in enumerate(weights):
        halos = exchange([c] * 4)
        result = call(
            coarse_kernel,
            [halos[b] for b in COARSE]
            + [coarse_left, c, correction, coarse_high, coarse_low, coarse_inverse],
            [small] if i == 1 else [small] * 3, weights=weight, last=i == 1,
        )
        correction = result[0]
        if i == 0:
            coarse_left, c = result[1:]
    halos = exchange([correction] * 4)
    left, new, iterate, correction_out = call(
        spread_kernel,
        [table, correction, onehot, iterate, leftover, inverse, spread_high, spread_low],
        [field, field, field, small], (), "s", "VV", flops=flops, **dims,
    )
    residual, update, *payloads = received(halos, left, new, None, "spread", (names,))
    halos = exchange(payloads)
    left, new, iterate = local(update, residual, iterate, weights[0])
    residual, update, *payloads = received(halos, left, new, weights[0])
    halos = exchange(payloads)
    left, new, iterate = local(update, residual, iterate, weights[1], "last")
    result = received(halos, left, new, weights[1], "last")
    return (result[0], correction_out)


def solution(mesh):
    placed = (
        P(None, AXES),
        P(None, AXES),
        P(AXES, None, None, None),
        P(AXES, None),
        P(AXES, None),
        P(AXES),
        P(AXES, None, None, None),
    )
    return jax.shard_map(
        local_program,
        mesh=mesh,
        in_specs=placed,
        out_specs=(P(None, AXES), P(None, AXES)),
        check_vma=False,
    )
```

```python
import functools

import jax
import jax.numpy as jnp
import numpy as np
from jax import lax
from jax.experimental import pallas as pl
from jax.experimental.pallas import tpu as pltpu
from jax.sharding import PartitionSpec as P

center_value = 1.1
radius_value = 0.9
AXES = ("span", "stream")
STEPS = ((0,), (1, 2, 3))
AHEAD = 3
COARSE = (3, 2, 1, 0)
CHUNK = 4
VMEM_LIMIT = 16 * 1024 * 1024
f32 = jnp.float32
bf16 = jnp.bfloat16
i32 = jnp.int32


def chebyshev_weights():
    weights = []
    old = radius_value / center_value
    for _ in range(2):
        now = 1.0 / (2.0 * center_value / radius_value - old)
        weights.append((now * old, 2.0 * now / radius_value))
        old = now
    return weights


def directions(s, t, n_span, n_stream, choose):
    span_even, span_odd = choose((s & 1) == 0, 1, 0), choose((s & 1) == 0, 0, 1)
    stream_even, stream_odd = choose((t & 1) == 0, 3, 2), choose((t & 1) == 0, 2, 3)
    end_s = (s == 0) | (s == n_span - 1)
    ahead = (((t + 1) >> 1) & 1) == 0
    return (
        choose(ahead, stream_odd, span_even),
        choose(ahead, span_even, choose(end_s, stream_odd, span_odd)),
        choose(ahead | end_s, span_odd, stream_odd),
        stream_even,
    )


def exchanges(n_span, n_stream):
    steps = ((-1, 0), (1, 0), (0, -1), (0, 1))
    partners = [{} for _ in range(4)]
    for s in range(n_span):
        for t in range(n_stream):
            way = directions(
                np.int32(s), np.int32(t), n_span, n_stream, lambda c, a, b: int(a if c else b)
            )
            for number in range(4):
                other_s, other_t = s + steps[way[number]][0], t + steps[way[number]][1]
                if 0 <= other_s < n_span and 0 <= other_t < n_stream:
                    partners[number][s, t] = (other_s, other_t)
    result = []
    for found in partners:
        idle = [(s, t) for s in range(n_span) for t in range(n_stream) if (s, t) not in found]
        while idle:
            s, t = idle.pop(0)
            other = min(
                idle,
                key=lambda o: (o != (s, t ^ 1), o[0] != s, abs(o[0] - s) + abs(o[1] - t)),
                default=(s, t),
            )
            if other in idle:
                idle.remove(other)
            found[s, t], found[other] = other, (s, t)
        result.append(
            [(s * n_stream + t, o[0] * n_stream + o[1]) for (s, t), o in sorted(found.items())]
        )
    return result


def place_in_mesh():
    s, t = lax.axis_index("span"), lax.axis_index("stream")
    n_span, n_stream = lax.axis_size("span"), lax.axis_size("stream")
    ways = directions(s, t, n_span, n_stream, jnp.where)
    there = [
        jnp.where(
            way < 2,
            jnp.where(way == 0, s > 0, s < n_span - 1),
            jnp.where(way == 2, t > 0, t < n_stream - 1),
        )
        for way in ways
    ]
    return ways, there


def dot_nt(a, b):
    return lax.dot_general(a, b, (((1,), (1,)), ((), ())), preferred_element_type=f32)


def dot_nn(a, b):
    return lax.dot_general(a, b, (((1,), (0,)), ((), ())), preferred_element_type=f32)


def high_low(x):
    high = x.astype(bf16)
    return high, (x - high.astype(f32)).astype(bf16)


def stacked(x):
    return jnp.concatenate(high_low(x), axis=0)


def halves(x):
    rows = x.shape[0] // 2
    return x[:rows] + x[rows:]


def block(index, size):
    return pl.ds(pl.multiple_of(index * size, size), size)


class Table:
    def __init__(self, blocks, count, slots):
        self.blocks, self.count, self.slots = blocks, count, slots
        self.capacity = blocks * (count - 1) + CHUNK
        self.columns = 4 * slots
        self.home = self.columns + blocks * count
        self.counts = self.home + 5
        self.entries = self.counts + 5
        self.length = self.entries + 5 * self.capacity

    def direction(self, slot):
        if self.slots & (self.slots - 1) == 0:
            return slot >> (self.slots.bit_length() - 1)
        return lax.div(slot, self.slots)

    def code(self, which, row, slot):
        return (which << 16) | (row << 8) | slot


def pack(table, field, outs, size, slots):
    for buffer in range(4):
        for h in range(slots):
            source = table[buffer * slots + h]
            outs[buffer][:, h * size : (h + 1) * size] = field[:, block(source, size)]


def load_kernel(
    guess, lists, columns, groups, o0, o1, o2, o3, field, lists_out, columns_out, names, sems, *, size, slots
):
    copies = [
        pltpu.make_async_copy(source, target, sems.at[i])
        for i, (source, target) in enumerate(
            ((lists, lists_out), (guess, field), (groups, names), (columns, columns_out))
        )
    ]
    for copy in copies:
        copy.start()
    ways, _ = place_in_mesh()
    for copy in copies:
        copy.wait()
    rows = field.shape[0]
    for buffer, out in enumerate((o0, o1, o2, o3)):
        direction = ways[buffer]
        for h in range(slots):
            at = block(lists_out[0, direction * slots + h], size)
            out[0:rows, h * size : (h + 1) * size] = field[:, at]
            out[rows : rows + 8, h * size : (h + 1) * size] = jnp.broadcast_to(
                names[:, at].astype(f32), (8, size)
            )


def split_field(field, wide, size):
    rows, width = field.shape
    high, low = high_low(field[...])
    wide[0:rows, 0:width] = high
    wide[rows : 2 * rows, 0:width] = low
    wide[0 : 2 * rows, width : width + size] = jnp.zeros((2 * rows, size), bf16)


def local_rows(table, lay, matrix, wide, g, size, rows):
    parts = [wide[0:rows, g * size : (g + 1) * size]]
    for k in range(1, lay.count):
        parts.append(wide[0:rows, block(table[lay.columns + g * lay.count + k], size)])
    pieces = [matrix[g * lay.count + k] for k in range(lay.count)]
    return dot_nt(jnp.concatenate(parts, axis=1), jnp.concatenate(pieces, axis=1))


def local_block(table, lay, matrix, wide, g, size, rows):
    return halves(local_rows(table, lay, matrix, wide, g, size, 2 * rows))


def diagonal_row(matrix, same):
    return jnp.sum(jnp.where(same, matrix.astype(f32), 0.0), axis=0, keepdims=True)


def square_mask(size):
    return lax.broadcasted_iota(i32, (size, size), 0) == lax.broadcasted_iota(
        i32, (size, size), 1
    )


def build_table(lists, columns, table, lay):
    ways, there = place_in_mesh()
    for buffer in range(4):
        direction = ways[buffer]
        table[lay.home + direction] = jnp.where(there[buffer], buffer, 4)
        for h in range(lay.slots):
            table[buffer * lay.slots + h] = lists[0, direction * lay.slots + h]
    table[lay.home + 4] = 4
    for buffer in range(5):
        table[lay.counts + buffer] = 0
    for g in range(lay.blocks):
        table[lay.columns + g * lay.count] = columns[0, g]
        for k in range(1, lay.count):
            column = columns[k, g]
            table[lay.columns + g * lay.count + k] = jnp.minimum(column, lay.blocks)
            slot = jnp.maximum(column - lay.blocks, 0)
            direction = jnp.where(column < lay.blocks, 4, lay.direction(slot))
            buffer = table[lay.home + direction]
            found = table[lay.counts + buffer]
            table[lay.entries + buffer * lay.capacity + found] = lay.code(
                g * lay.count + k, g, slot - lay.direction(slot) * lay.slots
            )
            table[lay.counts + buffer] = found + 1
    for buffer in range(4):
        found = table[lay.counts + buffer]
        for i in range(CHUNK):
            table[lay.entries + buffer * lay.capacity + found + i] = lay.slots


def sweep_weights(weights, inverse):
    if weights is None:
        return None, inverse[0:1, :] / center_value
    return weights[0], weights[1] * inverse[0:1, :]


def begin_sweep(left, update, iterate, inverse, new, weights, mode, onehot=None):
    if mode == "restrict":
        new[...] = halves(dot_nt(stacked(left[...]), onehot[...]))
        return
    a, b = sweep_weights(weights, inverse)
    change = b * left[...] if a is None else a * update[...] + b * left[...]
    new[...] = iterate[...] + change if mode == "last" else change


def first_kernel(
    lists, columns, field, target, source, left, new, table, inverse, matrix, wide, right, sems, *, size, lay, parts
):
    per = matrix.shape[0] // parts
    copies = [
        pltpu.make_async_copy(
            source.at[pl.ds(i * per, per)], matrix.at[pl.ds(i * per, per)], sems.at[i]
        )
        for i in range(parts)
    ]
    copies.append(pltpu.make_async_copy(target, right, sems.at[parts]))
    copies[parts].start()
    for copy in copies[:AHEAD]:
        copy.start()
    split_field(field, wide, size)
    build_table(lists, columns, table, lay)
    copies[parts].wait()
    same = square_mask(size)
    for g in range(lay.blocks):
        if g % (lay.blocks // parts) == 0:
            part = g // (lay.blocks // parts)
            copies[part].wait()
            if part + AHEAD < parts:
                copies[part + AHEAD].start()
        at = slice(g * size, (g + 1) * size)
        left[:, at] = right[:, at] - local_block(table, lay, matrix, wide, g, size, left.shape[0])
        inverse[:, at] = jnp.broadcast_to(
            1.0 / diagonal_row(matrix[g * lay.count], same), (8, size)
        )
    begin_sweep(left, None, None, inverse, new, None, "plain")


def local_kernel(table, update, residual, iterate, inverse, matrix, *refs, size, lay, weights, mode):
    refs = list(refs)
    onehot = refs.pop(0) if mode == "restrict" else None
    left, new, iterate_out, wide = refs
    split_field(update, wide, size)
    for g in range(lay.blocks):
        at = slice(g * size, (g + 1) * size)
        left[:, at] = residual[:, at] - local_block(table, lay, matrix, wide, g, size, left.shape[0])
    iterate_out[...] = iterate[...] + update[...]
    begin_sweep(left, update, iterate_out, inverse, new, weights, mode, onehot)


def turn_received(table, lay, matrix, turned, size):
    identity = jnp.where(square_mask(size), 1.0, 0.0).astype(bf16)

    def group(buffer, start):
        for i in range(CHUNK):
            which = table[lay.entries + buffer * lay.capacity + start + i] >> 16
            turned[which] = dot_nt(identity, matrix[which]).astype(bf16)

    for buffer in range(4):
        group(buffer, 0)

        def more(c, carry, buffer=buffer):
            group(buffer, c * CHUNK)
            return carry

        lax.fori_loop(1, (table[lay.counts + buffer] + CHUNK - 1) // CHUNK, more, 0)


def local_and_coarse_kernel(
    table, update, residual, iterate, inverse, matrix, groups, coarse, h0, h1, h2, h3,
    left, new, iterate_out, turned, onehot, names, coarse_high, coarse_low, coarse_inverse, wide, brought, cells, sems, *, size, lay, weights,
):
    copies = [
        pltpu.make_async_copy(coarse, brought, sems.at[0]),
        pltpu.make_async_copy(groups, cells, sems.at[1]),
    ]
    for copy in copies:
        copy.start()
    local_kernel(
        table, update, residual, iterate, inverse, matrix, left, new, iterate_out, wide,
        size=size, lay=lay, weights=weights, mode="plain",
    )
    turn_received(table, lay, matrix, turned, size)
    width = lay.slots * size
    rows = update.shape[0]
    number = lax.broadcasted_iota(i32, (size, width), 0).astype(f32)
    for buffer, received in enumerate((h0, h1, h2, h3)):
        names[:, buffer * width : (buffer + 1) * width] = jnp.where(
            number == received[rows : rows + 1, :], 1.0, 0.0
        ).astype(bf16)
    for copy in copies:
        copy.wait()
    onehot[...] = jnp.where(
        lax.broadcasted_iota(i32, onehot.shape, 0) == cells[...], 1.0, 0.0
    ).astype(bf16)
    coarse_inverse[...] = jnp.broadcast_to(
        1.0 / diagonal_row(brought[0], square_mask(size)), (8, size)
    )
    ways, there = place_in_mesh()
    for k in range(5):
        if k == 0:
            piece = brought[0]
        else:
            piece = jnp.where(there[k - 1], brought[1 + ways[k - 1]], 0.0)
        high, low = high_low(piece)
        coarse_high[:, k * size : (k + 1) * size] = high
        coarse_low[:, k * size : (k + 1) * size] = low


def put_halo(wide, place, x, size):
    rows, width = x.shape
    start = place * (width + size)
    high, low = high_low(x)
    wide[0:rows, start : start + width] = high
    wide[rows : 2 * rows, start : start + width] = low
    wide[:, start + width : start + width + size] = jnp.zeros((2 * rows, size), bf16)


def put_halos(wide, halos, buffers, names, rows, lay, size):
    for place, (buffer, received) in enumerate(zip(buffers, halos)):
        x = received[0:rows, :]
        if names is not None:
            width = lay.slots * size
            chosen = names[:, buffer * width : (buffer + 1) * width]
            x = halves(dot_nn(stacked(x), chosen))
        put_halo(wide, place, x, size)


def entry_product(code, matrix, wide, place, lay, size, dot):
    which, row, slot = code >> 16, (code >> 8) & 255, code & 255
    at = block(place * (lay.slots + 1) + slot, size)
    return block(row, size), halves(dot(wide[:, at], matrix[which]))


def for_received(table, lay, buffers, matrix, wide, size, dot, use):
    def group(members):
        use(
            [
                entry_product(
                    table[lay.entries + buffer * lay.capacity + i],
                    matrix, wide, place, lay, size, dot,
                )
                for place, buffer, i in members
            ]
        )

    group([(p, b, i) for p, b in enumerate(buffers) for i in range(CHUNK)])
    for place, buffer in enumerate(buffers):

        def more(c, carry, place=place, buffer=buffer):
            group([(place, buffer, c * CHUNK + i) for i in range(CHUNK)])
            return carry

        chunks = (table[lay.counts + buffer] + CHUNK - 1) // CHUNK
        lax.fori_loop(1, chunks, more, 0)


def received_kernel(table, left_in, new_in, inverse, matrix, *refs, size, lay, weights, mode, buffers, final, turned):
    refs = list(refs)
    halos, refs = refs[: len(buffers)], refs[len(buffers) :]
    rows = left_in.shape[0]
    names = refs.pop(0) if mode == "spread" else None
    if mode == "restrict":
        onehot, coarse_inverse = refs[:2]
        refs = refs[2:]
    wide, scaled = refs[-2:]
    left, new = refs[:2]
    if mode == "last" and final:
        new = refs[0]
        new[...] = new_in[...]
    put_halos(wide, halos, buffers, names, rows, lay, size)
    if mode != "restrict":
        scaled[0:1, :] = sweep_weights(weights, inverse)[1]

    def use(found):
        for at, product in found:
            if mode != "last":
                left[:, at] = left[:, at] - product
            if mode != "restrict":
                new[:, at] = new[:, at] - scaled[0:1, at] * product
        if mode == "restrict":
            new[...] = new[...] - sum(
                halves(dot_nt(stacked(product), onehot[:, at])) for at, product in found
            )

    for_received(table, lay, buffers, matrix, wide, size, dot_nn if turned else dot_nt, use)
    if not final or mode == "last":
        return
    if mode == "restrict":
        refs[2][...] = coarse_inverse[0:1, :] * new[...] / center_value
    else:
        pack(table, new, refs[2:6], size, lay.slots)


def coarse_kernel(
    h0, h1, h2, h3, residual, update, iterate, coarse_high, coarse_low, coarse_inverse, *outs, weights, last
):
    c = update[...]
    rows = c.shape[0]
    received = dict(zip(COARSE, (h0, h1, h2, h3)))
    high, low = high_low(jnp.concatenate([c] + [received[b][...] for b in range(4)], axis=1))
    product = halves(dot_nt(jnp.concatenate([high, low], axis=0), coarse_high[...]))
    left = residual[...] - (product + dot_nt(high, coarse_low[...]))
    new = weights[0] * c + weights[1] * coarse_inverse[0:1, :] * left
    outs[0][...] = iterate[...] + new
    if not last:
        outs[1][...] = left
        outs[2][...] = new


def local_and_spread_kernel(
    table, update, residual, iterate, inverse, matrix, onehot, left, new, iterate_out, high, low, wide, *, size, lay, weights
):
    local_kernel(
        table, update, residual, iterate, inverse, matrix, left, new, iterate_out, wide,
        size=size, lay=lay, weights=weights, mode="plain",
    )
    width = onehot.shape[1]
    wide[0:size, 0:width] = onehot[...]
    wide[0:size, width : width + size] = jnp.zeros((size, size), bf16)
    for g in range(lay.blocks):
        at = slice(g * size, (g + 1) * size)
        high[:, at], low[:, at] = high_low(
            local_rows(table, lay, matrix, wide, g, size, size)
        )


def spread_kernel(
    table, correction, onehot, iterate, leftover, inverse, spread_high, spread_low, left, new, second, correction_out, *, size, lay
):
    rows = correction.shape[0]
    both = stacked(correction[...])
    second[...] = iterate[...] + halves(dot_nn(both, onehot[...]))
    product = halves(dot_nn(both, spread_high[...])) + dot_nn(both[:rows], spread_low[...])
    left[...] = leftover[...] - product
    begin_sweep(left, None, None, inverse, new, None, "plain")
    correction_out[...] = correction[...]


def local_program(
    right_side, start_guess, fine_matrix, fine_columns, send_lists, aggregates, coarse_matrix
):
    perms = exchanges(lax.axis_size("span"), lax.axis_size("stream"))
    rows, width = right_side.shape
    blocks, count, size, _ = fine_matrix.shape
    slots = send_lists.shape[1] // 4
    halo_width = slots * size
    lay = Table(blocks, count, slots)
    groups = aggregates.reshape(1, width)
    stored = fine_matrix.reshape(blocks * count, size, size)
    coarse = coarse_matrix.reshape(coarse_matrix.shape[1:])
    weights = chebyshev_weights()
    parts = 4 if blocks % 4 == 0 else 1

    spaces = {
        "v": pl.BlockSpec(memory_space=pltpu.VMEM),
        "s": pl.BlockSpec(memory_space=pltpu.SMEM),
        "h": pl.BlockSpec(memory_space=pltpu.HBM),
    }

    def call(kernel, ins, outs, scratch=(), where="", kept="", aliases=None, flops=0, **named):
        where = where + "v" * (len(ins) - len(where))
        kept = kept + "v" * (len(outs) - len(kept))
        fixed = {"h": pltpu.HBM, "V": pltpu.VMEM}
        ins = [
            pltpu.with_memory_space_constraint(x, fixed[c]) if c in fixed else x
            for x, c in zip(ins, where)
        ]
        forms = {
            "v": jax.ShapeDtypeStruct,
            "V": pltpu.MemorySpace.VMEM,
            "s": pltpu.MemorySpace.SMEM,
        }
        return pl.pallas_call(
            functools.partial(kernel, **named),
            out_shape=[forms[c](shape, kind) for c, (shape, kind) in zip(kept, outs)],
            in_specs=[spaces[c.lower()] for c in where],
            out_specs=[spaces[c.lower()] for c in kept],
            scratch_shapes=list(scratch),
            input_output_aliases=aliases or {},
            compiler_params=pltpu.CompilerParams(vmem_limit_bytes=VMEM_LIMIT),
            cost_estimate=pl.CostEstimate(
                flops=flops, bytes_accessed=4 * 1024 * 1024, transcendentals=0
            ),
        )(*ins)

    def exchange(payloads):
        return [lax.ppermute(x, AXES, perm) for x, perm in zip(payloads, perms)]

    field = ((rows, width), f32)
    halo = ((rows, halo_width), f32)
    small = ((rows, size), f32)
    wide_local = pltpu.VMEM((2 * rows, width + size), bf16)
    wide_spread = pltpu.VMEM((max(2 * rows, size), width + size), bf16)
    flops = 2 * 2 * rows * blocks * count * size * size
    dims = {"size": size, "lay": lay}

    def received(halos, left, new, weight, mode="plain", extra=()):
        blocks_in = matrix if turned is None else turned
        for step, buffers in enumerate(STEPS):
            final = step == len(STEPS) - 1
            outs, kept = [field, small if mode == "restrict" else field], "VV"
            aliases = {1: 0, 2: 1}
            if mode == "last" and final:
                outs, kept, aliases = [field], "v", None
            elif mode == "restrict" and final:
                outs.append(small)
            elif final:
                outs += [halo] * 4
            result = call(
                received_kernel,
                [table, left, new, inverse, blocks_in] + [halos[b] for b in buffers] + list(extra),
                outs,
                [
                    pltpu.VMEM((2 * rows, len(buffers) * (halo_width + size)), bf16),
                    pltpu.VMEM((8, width), f32),
                ],
                "sVV", kept, aliases, flops=flops * len(buffers) // 20,
                weights=weight, mode=mode, buffers=buffers, final=final,
                turned=turned is not None, **dims,
            )
            left, new = result[0], result[1] if len(result) > 1 else None
        return result

    def local(update, residual, iterate, weight, mode="plain", extra=()):
        return call(
            local_kernel, [table, update, residual, iterate, inverse, matrix] + list(extra),
            [field, small if mode == "restrict" else field, field],
            [wide_local], "s", "VV", flops=flops, weights=weight, mode=mode, **dims,
        )

    *payloads, guess, lists, columns = call(
        load_kernel,
        [start_guess, send_lists, fine_columns.T, groups],
        [((rows + 8, halo_width), f32)] * 4
        + [field, (send_lists.shape, i32), (fine_columns.shape[::-1], i32)],
        [pltpu.VMEM((1, width), i32), pltpu.SemaphoreType.DMA((4,))],
        "hhhh", "vvvvvss", size=size, slots=slots,
    )
    first_halos = halos = exchange(payloads)
    left, new, table, inverse, matrix = call(
        first_kernel,
        [lists, columns, guess, right_side, stored],
        [field, field, ((lay.length,), i32), ((8, width), f32), (stored.shape, bf16)],
        [wide_local, pltpu.VMEM(*field), pltpu.SemaphoreType.DMA((parts + 1,))],
        "ssvhh", "VVs", flops=flops, parts=parts, **dims,
    )
    turned = None
    residual, update, *payloads = received(halos, left, new, None)
    halos = exchange(payloads)
    left, new, iterate, turned, onehot, names, coarse_high, coarse_low, coarse_inverse = call(
        local_and_coarse_kernel,
        [table, update, residual, guess, inverse, matrix, groups, coarse] + first_halos,
        [
            field,
            field,
            field,
            (stored.shape, bf16),
            ((size, width), bf16),
            ((size, 4 * halo_width), bf16),
            ((size, 5 * size), bf16),
            ((size, 5 * size), bf16),
            ((8, size), f32),
        ],
        [
            wide_local,
            pltpu.VMEM(coarse.shape, f32),
            pltpu.VMEM((1, width), i32),
            pltpu.SemaphoreType.DMA((2,)),
        ],
        "svvvvvhh", "VV", flops=flops, weights=weights[0], **dims,
    )
    residual, update, *payloads = received(halos, left, new, weights[0])
    halos = exchange(payloads)
    left, new, iterate, spread_high, spread_low = call(
        local_and_spread_kernel, [table, update, residual, iterate, inverse, matrix, onehot],
        [field, field, field, ((size, width), bf16), ((size, width), bf16)],
        [wide_spread], "s", "VV", flops=flops, weights=weights[1], **dims,
    )
    residual, update, *payloads = received(halos, left, new, weights[1])
    halos = exchange(payloads)
    left, new, iterate = local(update, residual, iterate, None, "restrict", (onehot,))
    leftover, coarse_left, c = received(
        halos, left, new, None, "restrict", (onehot, coarse_inverse)
    )
    correction = c
    for i, weight in enumerate(weights):
        halos = exchange([c] * 4)
        result = call(
            coarse_kernel,
            [halos[b] for b in COARSE]
            + [coarse_left, c, correction, coarse_high, coarse_low, coarse_inverse],
            [small] if i == 1 else [small] * 3, weights=weight, last=i == 1,
        )
        correction = result[0]
        if i == 0:
            coarse_left, c = result[1:]
    halos = exchange([correction] * 4)
    left, new, iterate, correction_out = call(
        spread_kernel,
        [table, correction, onehot, iterate, leftover, inverse, spread_high, spread_low],
        [field, field, field, small], (), "s", "VV", flops=flops, **dims,
    )
    residual, update, *payloads = received(halos, left, new, None, "spread", (names,))
    halos = exchange(payloads)
    left, new, iterate = local(update, residual, iterate, weights[0])
    residual, update, *payloads = received(halos, left, new, weights[0])
    halos = exchange(payloads)
    left, new, iterate = local(update, residual, iterate, weights[1], "last")
    result = received(halos, left, new, weights[1], "last")
    return (result[0], correction_out)


def solution(mesh):
    placed = (
        P(None, AXES),
        P(None, AXES),
        P(AXES, None, None, None),
        P(AXES, None),
        P(AXES, None),
        P(AXES),
        P(AXES, None, None, None),
    )
    return jax.shard_map(
        local_program,
        mesh=mesh,
        in_specs=placed,
        out_specs=(P(None, AXES), P(None, AXES)),
        check_vma=False,
    )
```

```python
import functools

import jax
import jax.numpy as jnp
import numpy as np
from jax import lax
from jax.experimental import pallas as pl
from jax.experimental.pallas import tpu as pltpu
from jax.sharding import PartitionSpec as P

center_value = 1.1
radius_value = 0.9
AXES = ("span", "stream")
STEPS = ((0,), (1, 2, 3))
SPREAD_STEPS = ((0,), (3, 2, 1))
AHEAD = 3
COARSE = (3, 2, 1, 0)
CHUNK = 4
VMEM_LIMIT = 16 * 1024 * 1024
f32 = jnp.float32
bf16 = jnp.bfloat16
i32 = jnp.int32


def chebyshev_weights():
    weights = []
    old = radius_value / center_value
    for _ in range(2):
        now = 1.0 / (2.0 * center_value / radius_value - old)
        weights.append((now * old, 2.0 * now / radius_value))
        old = now
    return weights


def directions(s, t, n_span, n_stream, choose):
    span_even, span_odd = choose((s & 1) == 0, 1, 0), choose((s & 1) == 0, 0, 1)
    stream_even, stream_odd = choose((t & 1) == 0, 3, 2), choose((t & 1) == 0, 2, 3)
    end_s = (s == 0) | (s == n_span - 1)
    ahead = (((t + 1) >> 1) & 1) == 0
    return (
        choose(ahead, stream_odd, span_even),
        choose(ahead, span_even, choose(end_s, stream_odd, span_odd)),
        choose(ahead | end_s, span_odd, stream_odd),
        stream_even,
    )


def exchanges(n_span, n_stream):
    steps = ((-1, 0), (1, 0), (0, -1), (0, 1))
    partners = [{} for _ in range(4)]
    for s in range(n_span):
        for t in range(n_stream):
            way = directions(
                np.int32(s), np.int32(t), n_span, n_stream, lambda c, a, b: int(a if c else b)
            )
            for number in range(4):
                other_s, other_t = s + steps[way[number]][0], t + steps[way[number]][1]
                if 0 <= other_s < n_span and 0 <= other_t < n_stream:
                    partners[number][s, t] = (other_s, other_t)
    result = []
    for found in partners:
        idle = [(s, t) for s in range(n_span) for t in range(n_stream) if (s, t) not in found]
        while idle:
            s, t = idle.pop(0)
            other = min(
                idle,
                key=lambda o: (o != (s, t ^ 1), o[0] != s, abs(o[0] - s) + abs(o[1] - t)),
                default=(s, t),
            )
            if other in idle:
                idle.remove(other)
            found[s, t], found[other] = other, (s, t)
        result.append(
            [(s * n_stream + t, o[0] * n_stream + o[1]) for (s, t), o in sorted(found.items())]
        )
    return result


def place_in_mesh():
    s, t = lax.axis_index("span"), lax.axis_index("stream")
    n_span, n_stream = lax.axis_size("span"), lax.axis_size("stream")
    ways = directions(s, t, n_span, n_stream, jnp.where)
    there = [
        jnp.where(
            way < 2,
            jnp.where(way == 0, s > 0, s < n_span - 1),
            jnp.where(way == 2, t > 0, t < n_stream - 1),
        )
        for way in ways
    ]
    return ways, there


def dot_nt(a, b):
    return lax.dot_general(a, b, (((1,), (1,)), ((), ())), preferred_element_type=f32)


def dot_nn(a, b):
    return lax.dot_general(a, b, (((1,), (0,)), ((), ())), preferred_element_type=f32)


def high_low(x):
    high = x.astype(bf16)
    return high, (x - high.astype(f32)).astype(bf16)


def stacked(x):
    return jnp.concatenate(high_low(x), axis=0)


def halves(x):
    rows = x.shape[0] // 2
    return x[:rows] + x[rows:]


def block(index, size):
    return pl.ds(pl.multiple_of(index * size, size), size)


class Table:
    def __init__(self, blocks, count, slots):
        self.blocks, self.count, self.slots = blocks, count, slots
        self.capacity = blocks * (count - 1) + CHUNK
        self.columns = 4 * slots
        self.home = self.columns + blocks * count
        self.counts = self.home + 5
        self.entries = self.counts + 5
        self.length = self.entries + 5 * self.capacity

    def direction(self, slot):
        if self.slots & (self.slots - 1) == 0:
            return slot >> (self.slots.bit_length() - 1)
        return lax.div(slot, self.slots)

    def code(self, which, row, slot):
        return (which << 16) | (row << 8) | slot


def pack(table, field, outs, size, slots):
    for buffer in range(4):
        for h in range(slots):
            source = table[buffer * slots + h]
            outs[buffer][:, h * size : (h + 1) * size] = field[:, block(source, size)]


def load_kernel(
    guess, lists, columns, groups, o0, o1, o2, o3, field, lists_out, columns_out, names, sems, *, size, slots
):
    copies = [
        pltpu.make_async_copy(source, target, sems.at[i])
        for i, (source, target) in enumerate(
            ((lists, lists_out), (guess, field), (groups, names), (columns, columns_out))
        )
    ]
    for copy in copies:
        copy.start()
    ways, _ = place_in_mesh()
    for copy in copies:
        copy.wait()
    rows = field.shape[0]
    for buffer, out in enumerate((o0, o1, o2, o3)):
        direction = ways[buffer]
        for h in range(slots):
            at = block(lists_out[0, direction * slots + h], size)
            out[0:rows, h * size : (h + 1) * size] = field[:, at]
            out[rows : rows + 8, h * size : (h + 1) * size] = jnp.broadcast_to(
                names[:, at].astype(f32), (8, size)
            )


def split_field(field, wide, size):
    rows, width = field.shape
    high, low = high_low(field[...])
    wide[0:rows, 0:width] = high
    wide[rows : 2 * rows, 0:width] = low
    wide[0 : 2 * rows, width : width + size] = jnp.zeros((2 * rows, size), bf16)


def local_rows(table, lay, matrix, wide, g, size, rows):
    parts = [wide[0:rows, g * size : (g + 1) * size]]
    for k in range(1, lay.count):
        parts.append(wide[0:rows, block(table[lay.columns + g * lay.count + k], size)])
    pieces = [matrix[g * lay.count + k] for k in range(lay.count)]
    return dot_nt(jnp.concatenate(parts, axis=1), jnp.concatenate(pieces, axis=1))


def local_block(table, lay, matrix, wide, g, size, rows):
    return halves(local_rows(table, lay, matrix, wide, g, size, 2 * rows))


def diagonal_row(matrix, same):
    return jnp.sum(jnp.where(same, matrix.astype(f32), 0.0), axis=0, keepdims=True)


def square_mask(size):
    return lax.broadcasted_iota(i32, (size, size), 0) == lax.broadcasted_iota(
        i32, (size, size), 1
    )


def build_table(lists, columns, table, lay):
    ways, there = place_in_mesh()
    for buffer in range(4):
        direction = ways[buffer]
        table[lay.home + direction] = jnp.where(there[buffer], buffer, 4)
        for h in range(lay.slots):
            table[buffer * lay.slots + h] = lists[0, direction * lay.slots + h]
    table[lay.home + 4] = 4
    for buffer in range(5):
        table[lay.counts + buffer] = 0
    for g in range(lay.blocks):
        table[lay.columns + g * lay.count] = columns[0, g]
        for k in range(1, lay.count):
            column = columns[k, g]
            table[lay.columns + g * lay.count + k] = jnp.minimum(column, lay.blocks)
            slot = jnp.maximum(column - lay.blocks, 0)
            direction = jnp.where(column < lay.blocks, 4, lay.direction(slot))
            buffer = table[lay.home + direction]
            found = table[lay.counts + buffer]
            table[lay.entries + buffer * lay.capacity + found] = lay.code(
                g * lay.count + k, g, slot - lay.direction(slot) * lay.slots
            )
            table[lay.counts + buffer] = found + 1
    for buffer in range(4):
        found = table[lay.counts + buffer]
        for i in range(CHUNK):
            table[lay.entries + buffer * lay.capacity + found + i] = lay.slots


def sweep_weights(weights, inverse):
    if weights is None:
        return None, inverse[0:1, :] / center_value
    return weights[0], weights[1] * inverse[0:1, :]


def begin_sweep(left, update, iterate, inverse, new, weights, mode, onehot=None):
    if mode == "restrict":
        new[...] = halves(dot_nt(stacked(left[...]), onehot[...]))
        return
    a, b = sweep_weights(weights, inverse)
    change = b * left[...] if a is None else a * update[...] + b * left[...]
    new[...] = iterate[...] + change if mode == "last" else change


def first_kernel(
    lists, columns, field, target, source, left, new, table, inverse, matrix, wide, right, sems, *, size, lay, parts
):
    per = matrix.shape[0] // parts
    copies = [
        pltpu.make_async_copy(
            source.at[pl.ds(i * per, per)], matrix.at[pl.ds(i * per, per)], sems.at[i]
        )
        for i in range(parts)
    ]
    copies.append(pltpu.make_async_copy(target, right, sems.at[parts]))
    copies[parts].start()
    for copy in copies[:AHEAD]:
        copy.start()
    split_field(field, wide, size)
    build_table(lists, columns, table, lay)
    copies[parts].wait()
    same = square_mask(size)
    for g in range(lay.blocks):
        if g % (lay.blocks // parts) == 0:
            part = g // (lay.blocks // parts)
            copies[part].wait()
            if part + AHEAD < parts:
                copies[part + AHEAD].start()
        at = slice(g * size, (g + 1) * size)
        left[:, at] = right[:, at] - local_block(table, lay, matrix, wide, g, size, left.shape[0])
        inverse[:, at] = jnp.broadcast_to(
            1.0 / diagonal_row(matrix[g * lay.count], same), (8, size)
        )
    begin_sweep(left, None, None, inverse, new, None, "plain")


def local_kernel(table, update, residual, iterate, inverse, matrix, *refs, size, lay, weights, mode):
    refs = list(refs)
    onehot = refs.pop(0) if mode == "restrict" else None
    left, new, iterate_out, wide = refs
    split_field(update, wide, size)
    for g in range(lay.blocks):
        at = slice(g * size, (g + 1) * size)
        left[:, at] = residual[:, at] - local_block(table, lay, matrix, wide, g, size, left.shape[0])
    iterate_out[...] = iterate[...] + update[...]
    begin_sweep(left, update, iterate_out, inverse, new, weights, mode, onehot)


def turn_received(table, lay, matrix, turned, size):
    identity = jnp.where(square_mask(size), 1.0, 0.0).astype(bf16)

    def group(buffer, start):
        for i in range(CHUNK):
            which = table[lay.entries + buffer * lay.capacity + start + i] >> 16
            turned[which] = dot_nt(identity, matrix[which]).astype(bf16)

    for buffer in range(4):
        group(buffer, 0)

        def more(c, carry, buffer=buffer):
            group(buffer, c * CHUNK)
            return carry

        lax.fori_loop(1, (table[lay.counts + buffer] + CHUNK - 1) // CHUNK, more, 0)


def local_and_coarse_kernel(
    table, update, residual, iterate, inverse, matrix, groups, coarse, h0, h1, h2, h3,
    left, new, iterate_out, turned, onehot, names, coarse_high, coarse_low, coarse_inverse, wide, brought, cells, sems, *, size, lay, weights,
):
    copies = [
        pltpu.make_async_copy(coarse, brought, sems.at[0]),
        pltpu.make_async_copy(groups, cells, sems.at[1]),
    ]
    for copy in copies:
        copy.start()
    local_kernel(
        table, update, residual, iterate, inverse, matrix, left, new, iterate_out, wide,
        size=size, lay=lay, weights=weights, mode="plain",
    )
    turn_received(table, lay, matrix, turned, size)
    width = lay.slots * size
    rows = update.shape[0]
    number = lax.broadcasted_iota(i32, (size, width), 0).astype(f32)
    for buffer, received in enumerate((h0, h1, h2, h3)):
        names[:, buffer * width : (buffer + 1) * width] = jnp.where(
            number == received[rows : rows + 1, :], 1.0, 0.0
        ).astype(bf16)
    for copy in copies:
        copy.wait()
    onehot[...] = jnp.where(
        lax.broadcasted_iota(i32, onehot.shape, 0) == cells[...], 1.0, 0.0
    ).astype(bf16)
    coarse_inverse[...] = jnp.broadcast_to(
        1.0 / diagonal_row(brought[0], square_mask(size)), (8, size)
    )
    ways, there = place_in_mesh()
    for k in range(5):
        if k == 0:
            piece = brought[0]
        else:
            piece = jnp.where(there[k - 1], brought[1 + ways[k - 1]], 0.0)
        high, low = high_low(piece)
        coarse_high[:, k * size : (k + 1) * size] = high
        coarse_low[:, k * size : (k + 1) * size] = low


def put_halo(wide, place, x, size):
    rows, width = x.shape
    start = place * (width + size)
    high, low = high_low(x)
    wide[0:rows, start : start + width] = high
    wide[rows : 2 * rows, start : start + width] = low
    wide[:, start + width : start + width + size] = jnp.zeros((2 * rows, size), bf16)


def put_halos(wide, halos, buffers, names, rows, lay, size):
    for place, (buffer, received) in enumerate(zip(buffers, halos)):
        x = received[0:rows, :]
        if names is not None:
            width = lay.slots * size
            chosen = names[:, buffer * width : (buffer + 1) * width]
            x = halves(dot_nn(stacked(x), chosen))
        put_halo(wide, place, x, size)


def entry_product(code, matrix, wide, place, lay, size, dot):
    which, row, slot = code >> 16, (code >> 8) & 255, code & 255
    at = block(place * (lay.slots + 1) + slot, size)
    return block(row, size), halves(dot(wide[:, at], matrix[which]))


def for_received(table, lay, buffers, matrix, wide, size, dot, use):
    def group(members):
        use(
            [
                entry_product(
                    table[lay.entries + buffer * lay.capacity + i],
                    matrix, wide, place, lay, size, dot,
                )
                for place, buffer, i in members
            ]
        )

    group([(p, b, i) for p, b in enumerate(buffers) for i in range(CHUNK)])
    for place, buffer in enumerate(buffers):

        def more(c, carry, place=place, buffer=buffer):
            group([(place, buffer, c * CHUNK + i) for i in range(CHUNK)])
            return carry

        chunks = (table[lay.counts + buffer] + CHUNK - 1) // CHUNK
        lax.fori_loop(1, chunks, more, 0)


def received_kernel(table, left_in, new_in, inverse, matrix, *refs, size, lay, weights, mode, buffers, final, turned):
    refs = list(refs)
    halos, refs = refs[: len(buffers)], refs[len(buffers) :]
    rows = left_in.shape[0]
    names = refs.pop(0) if mode == "spread" else None
    if mode == "restrict":
        onehot, coarse_inverse = refs[:2]
        refs = refs[2:]
    wide, scaled = refs[-2:]
    left, new = refs[:2]
    if mode == "last" and final:
        new = refs[0]
        new[...] = new_in[...]
    put_halos(wide, halos, buffers, names, rows, lay, size)
    if mode != "restrict":
        scaled[0:1, :] = sweep_weights(weights, inverse)[1]

    def use(found):
        for at, product in found:
            if mode != "last":
                left[:, at] = left[:, at] - product
            if mode != "restrict":
                new[:, at] = new[:, at] - scaled[0:1, at] * product
        if mode == "restrict":
            new[...] = new[...] - sum(
                halves(dot_nt(stacked(product), onehot[:, at])) for at, product in found
            )

    for_received(table, lay, buffers, matrix, wide, size, dot_nn if turned else dot_nt, use)
    if not final or mode == "last":
        return
    if mode == "restrict":
        refs[2][...] = coarse_inverse[0:1, :] * new[...] / center_value
    else:
        pack(table, new, refs[2:6], size, lay.slots)


def coarse_kernel(
    h0, h1, h2, h3, residual, update, iterate, coarse_high, coarse_low, coarse_inverse, *outs, weights, last
):
    c = update[...]
    rows = c.shape[0]
    received = dict(zip(COARSE, (h0, h1, h2, h3)))
    high, low = high_low(jnp.concatenate([c] + [received[b][...] for b in range(4)], axis=1))
    product = halves(dot_nt(jnp.concatenate([high, low], axis=0), coarse_high[...]))
    left = residual[...] - (product + dot_nt(high, coarse_low[...]))
    new = weights[0] * c + weights[1] * coarse_inverse[0:1, :] * left
    outs[0][...] = iterate[...] + new
    if not last:
        outs[1][...] = left
        outs[2][...] = new


def local_and_spread_kernel(
    table, update, residual, iterate, inverse, matrix, onehot, left, new, iterate_out, high, low, wide, *, size, lay, weights
):
    local_kernel(
        table, update, residual, iterate, inverse, matrix, left, new, iterate_out, wide,
        size=size, lay=lay, weights=weights, mode="plain",
    )
    width = onehot.shape[1]
    wide[0:size, 0:width] = onehot[...]
    wide[0:size, width : width + size] = jnp.zeros((size, size), bf16)
    for g in range(lay.blocks):
        at = slice(g * size, (g + 1) * size)
        high[:, at], low[:, at] = high_low(
            local_rows(table, lay, matrix, wide, g, size, size)
        )


def spread_kernel(
    table, correction, onehot, iterate, leftover, inverse, spread_high, spread_low, left, new, second, correction_out, *, size, lay
):
    rows = correction.shape[0]
    both = stacked(correction[...])
    second[...] = iterate[...] + halves(dot_nn(both, onehot[...]))
    product = halves(dot_nn(both, spread_high[...])) + dot_nn(both[:rows], spread_low[...])
    left[...] = leftover[...] - product
    begin_sweep(left, None, None, inverse, new, None, "plain")
    correction_out[...] = correction[...]


def local_program(
    right_side, start_guess, fine_matrix, fine_columns, send_lists, aggregates, coarse_matrix
):
    perms = exchanges(lax.axis_size("span"), lax.axis_size("stream"))
    rows, width = right_side.shape
    blocks, count, size, _ = fine_matrix.shape
    slots = send_lists.shape[1] // 4
    halo_width = slots * size
    lay = Table(blocks, count, slots)
    groups = aggregates.reshape(1, width)
    stored = fine_matrix.reshape(blocks * count, size, size)
    coarse = coarse_matrix.reshape(coarse_matrix.shape[1:])
    weights = chebyshev_weights()
    parts = 4 if blocks % 4 == 0 else 1

    spaces = {
        "v": pl.BlockSpec(memory_space=pltpu.VMEM),
        "s": pl.BlockSpec(memory_space=pltpu.SMEM),
        "h": pl.BlockSpec(memory_space=pltpu.HBM),
    }

    def call(kernel, ins, outs, scratch=(), where="", kept="", aliases=None, flops=0, **named):
        where = where + "v" * (len(ins) - len(where))
        kept = kept + "v" * (len(outs) - len(kept))
        fixed = {"h": pltpu.HBM, "V": pltpu.VMEM}
        ins = [
            pltpu.with_memory_space_constraint(x, fixed[c]) if c in fixed else x
            for x, c in zip(ins, where)
        ]
        forms = {
            "v": jax.ShapeDtypeStruct,
            "V": pltpu.MemorySpace.VMEM,
            "s": pltpu.MemorySpace.SMEM,
        }
        return pl.pallas_call(
            functools.partial(kernel, **named),
            out_shape=[forms[c](shape, kind) for c, (shape, kind) in zip(kept, outs)],
            in_specs=[spaces[c.lower()] for c in where],
            out_specs=[spaces[c.lower()] for c in kept],
            scratch_shapes=list(scratch),
            input_output_aliases=aliases or {},
            compiler_params=pltpu.CompilerParams(vmem_limit_bytes=VMEM_LIMIT),
            cost_estimate=pl.CostEstimate(
                flops=flops, bytes_accessed=4 * 1024 * 1024, transcendentals=0
            ),
        )(*ins)

    def exchange(payloads):
        return [lax.ppermute(x, AXES, perm) for x, perm in zip(payloads, perms)]

    field = ((rows, width), f32)
    halo = ((rows, halo_width), f32)
    small = ((rows, size), f32)
    wide_local = pltpu.VMEM((2 * rows, width + size), bf16)
    wide_spread = pltpu.VMEM((max(2 * rows, size), width + size), bf16)
    flops = 2 * 2 * rows * blocks * count * size * size
    dims = {"size": size, "lay": lay}

    def received(halos, left, new, weight, mode="plain", extra=()):
        blocks_in = matrix if turned is None else turned
        steps = SPREAD_STEPS if mode == "spread" else STEPS
        for step, buffers in enumerate(steps):
            final = step == len(steps) - 1
            outs, kept = [field, small if mode == "restrict" else field], "VV"
            aliases = {1: 0, 2: 1}
            if mode == "last" and final:
                outs, kept, aliases = [field], "v", None
            elif mode == "restrict" and final:
                outs.append(small)
            elif final:
                outs += [halo] * 4
            result = call(
                received_kernel,
                [table, left, new, inverse, blocks_in] + [halos[b] for b in buffers] + list(extra),
                outs,
                [
                    pltpu.VMEM((2 * rows, len(buffers) * (halo_width + size)), bf16),
                    pltpu.VMEM((8, width), f32),
                ],
                "sVV", kept, aliases, flops=flops * len(buffers) // 20,
                weights=weight, mode=mode, buffers=buffers, final=final,
                turned=turned is not None, **dims,
            )
            left, new = result[0], result[1] if len(result) > 1 else None
        return result

    def local(update, residual, iterate, weight, mode="plain", extra=()):
        return call(
            local_kernel, [table, update, residual, iterate, inverse, matrix] + list(extra),
            [field, small if mode == "restrict" else field, field],
            [wide_local], "s", "VV", flops=flops, weights=weight, mode=mode, **dims,
        )

    *payloads, guess, lists, columns = call(
        load_kernel,
        [start_guess, send_lists, fine_columns.T, groups],
        [((rows + 8, halo_width), f32)] * 4
        + [field, (send_lists.shape, i32), (fine_columns.shape[::-1], i32)],
        [pltpu.VMEM((1, width), i32), pltpu.SemaphoreType.DMA((4,))],
        "hhhh", "vvvvvss", size=size, slots=slots,
    )
    first_halos = halos = exchange(payloads)
    left, new, table, inverse, matrix = call(
        first_kernel,
        [lists, columns, guess, right_side, stored],
        [field, field, ((lay.length,), i32), ((8, width), f32), (stored.shape, bf16)],
        [wide_local, pltpu.VMEM(*field), pltpu.SemaphoreType.DMA((parts + 1,))],
        "ssvhh", "VVs", flops=flops, parts=parts, **dims,
    )
    turned = None
    residual, update, *payloads = received(halos, left, new, None)
    halos = exchange(payloads)
    left, new, iterate, turned, onehot, names, coarse_high, coarse_low, coarse_inverse = call(
        local_and_coarse_kernel,
        [table, update, residual, guess, inverse, matrix, groups, coarse] + first_halos,
        [
            field,
            field,
            field,
            (stored.shape, bf16),
            ((size, width), bf16),
            ((size, 4 * halo_width), bf16),
            ((size, 5 * size), bf16),
            ((size, 5 * size), bf16),
            ((8, size), f32),
        ],
        [
            wide_local,
            pltpu.VMEM(coarse.shape, f32),
            pltpu.VMEM((1, width), i32),
            pltpu.SemaphoreType.DMA((2,)),
        ],
        "svvvvvhh", "VV", flops=flops, weights=weights[0], **dims,
    )
    residual, update, *payloads = received(halos, left, new, weights[0])
    halos = exchange(payloads)
    left, new, iterate, spread_high, spread_low = call(
        local_and_spread_kernel, [table, update, residual, iterate, inverse, matrix, onehot],
        [field, field, field, ((size, width), bf16), ((size, width), bf16)],
        [wide_spread], "s", "VV", flops=flops, weights=weights[1], **dims,
    )
    residual, update, *payloads = received(halos, left, new, weights[1])
    halos = exchange(payloads)
    left, new, iterate = local(update, residual, iterate, None, "restrict", (onehot,))
    leftover, coarse_left, c = received(
        halos, left, new, None, "restrict", (onehot, coarse_inverse)
    )
    correction = c
    for i, weight in enumerate(weights):
        halos = exchange([c] * 4)
        result = call(
            coarse_kernel,
            [halos[b] for b in COARSE]
            + [coarse_left, c, correction, coarse_high, coarse_low, coarse_inverse],
            [small] if i == 1 else [small] * 3, weights=weight, last=i == 1,
        )
        correction = result[0]
        if i == 0:
            coarse_left, c = result[1:]
    halos = exchange([correction] * 4)
    left, new, iterate, correction_out = call(
        spread_kernel,
        [table, correction, onehot, iterate, leftover, inverse, spread_high, spread_low],
        [field, field, field, small], (), "s", "VV", flops=flops, **dims,
    )
    residual, update, *payloads = received(halos, left, new, None, "spread", (names,))
    halos = exchange(payloads)
    left, new, iterate = local(update, residual, iterate, weights[0])
    residual, update, *payloads = received(halos, left, new, weights[0])
    halos = exchange(payloads)
    left, new, iterate = local(update, residual, iterate, weights[1], "last")
    result = received(halos, left, new, weights[1], "last")
    return (result[0], correction_out)


def solution(mesh):
    placed = (
        P(None, AXES),
        P(None, AXES),
        P(AXES, None, None, None),
        P(AXES, None),
        P(AXES, None),
        P(AXES),
        P(AXES, None, None, None),
    )
    return jax.shard_map(
        local_program,
        mesh=mesh,
        in_specs=placed,
        out_specs=(P(None, AXES), P(None, AXES)),
        check_vma=False,
    )
```

```python
import functools

import jax
import jax.numpy as jnp
import numpy as np
from jax import lax
from jax.experimental import pallas as pl
from jax.experimental.pallas import tpu as pltpu
from jax.sharding import PartitionSpec as P

center_value = 1.1
radius_value = 0.9
AXES = ("span", "stream")
STEPS = ((0,), (1, 2, 3))
SPREAD_STEPS = ((0,), (3, 2, 1))
AHEAD = 3
COARSE = (3, 2, 1, 0)
CHUNK = 4
VMEM_LIMIT = 16 * 1024 * 1024
f32 = jnp.float32
bf16 = jnp.bfloat16
i32 = jnp.int32


def chebyshev_weights():
    weights = []
    old = radius_value / center_value
    for _ in range(2):
        now = 1.0 / (2.0 * center_value / radius_value - old)
        weights.append((now * old, 2.0 * now / radius_value))
        old = now
    return weights


def directions(s, t, n_span, n_stream, choose):
    span_even, span_odd = choose((s & 1) == 0, 1, 0), choose((s & 1) == 0, 0, 1)
    stream_even, stream_odd = choose((t & 1) == 0, 3, 2), choose((t & 1) == 0, 2, 3)
    end_s = (s == 0) | (s == n_span - 1)
    ahead = (((t + 1) >> 1) & 1) == 0
    return (
        choose(ahead, stream_odd, span_even),
        choose(ahead, span_even, choose(end_s, stream_odd, span_odd)),
        choose(ahead | end_s, span_odd, stream_odd),
        stream_even,
    )


def exchanges(n_span, n_stream):
    steps = ((-1, 0), (1, 0), (0, -1), (0, 1))
    partners = [{} for _ in range(4)]
    for s in range(n_span):
        for t in range(n_stream):
            way = directions(
                np.int32(s), np.int32(t), n_span, n_stream, lambda c, a, b: int(a if c else b)
            )
            for number in range(4):
                other_s, other_t = s + steps[way[number]][0], t + steps[way[number]][1]
                if 0 <= other_s < n_span and 0 <= other_t < n_stream:
                    partners[number][s, t] = (other_s, other_t)
    result = []
    for found in partners:
        idle = [(s, t) for s in range(n_span) for t in range(n_stream) if (s, t) not in found]
        while idle:
            s, t = idle.pop(0)
            other = min(
                idle,
                key=lambda o: (o != (s, t ^ 1), o[0] != s, abs(o[0] - s) + abs(o[1] - t)),
                default=(s, t),
            )
            if other in idle:
                idle.remove(other)
            found[s, t], found[other] = other, (s, t)
        result.append(
            [(s * n_stream + t, o[0] * n_stream + o[1]) for (s, t), o in sorted(found.items())]
        )
    return result


def place_in_mesh():
    s, t = lax.axis_index("span"), lax.axis_index("stream")
    n_span, n_stream = lax.axis_size("span"), lax.axis_size("stream")
    ways = directions(s, t, n_span, n_stream, jnp.where)
    there = [
        jnp.where(
            way < 2,
            jnp.where(way == 0, s > 0, s < n_span - 1),
            jnp.where(way == 2, t > 0, t < n_stream - 1),
        )
        for way in ways
    ]
    return ways, there


def dot_nt(a, b):
    return lax.dot_general(a, b, (((1,), (1,)), ((), ())), preferred_element_type=f32)


def dot_nn(a, b):
    return lax.dot_general(a, b, (((1,), (0,)), ((), ())), preferred_element_type=f32)


def high_low(x):
    high = x.astype(bf16)
    return high, (x - high.astype(f32)).astype(bf16)


def stacked(x):
    return jnp.concatenate(high_low(x), axis=0)


def halves(x):
    rows = x.shape[0] // 2
    return x[:rows] + x[rows:]


def block(index, size):
    return pl.ds(pl.multiple_of(index * size, size), size)


class Table:
    def __init__(self, blocks, count, slots):
        self.blocks, self.count, self.slots = blocks, count, slots
        self.capacity = blocks * (count - 1) + CHUNK
        self.columns = 4 * slots
        self.home = self.columns + blocks * count
        self.counts = self.home + 5
        self.entries = self.counts + 5
        self.length = self.entries + 5 * self.capacity

    def direction(self, slot):
        if self.slots & (self.slots - 1) == 0:
            return slot >> (self.slots.bit_length() - 1)
        return lax.div(slot, self.slots)

    def code(self, which, row, slot):
        return (which << 16) | (row << 8) | slot


def pack(table, field, outs, size, slots):
    for buffer in range(4):
        for h in range(slots):
            source = table[buffer * slots + h]
            outs[buffer][:, h * size : (h + 1) * size] = field[:, block(source, size)]


def load_kernel(
    guess, lists, columns, groups, o0, o1, o2, o3, field, lists_out, columns_out, names, sems, *, size, slots
):
    copies = [
        pltpu.make_async_copy(source, target, sems.at[i])
        for i, (source, target) in enumerate(
            ((lists, lists_out), (guess, field), (groups, names), (columns, columns_out))
        )
    ]
    for copy in copies:
        copy.start()
    ways, _ = place_in_mesh()
    for copy in copies:
        copy.wait()
    rows = field.shape[0]
    for buffer, out in enumerate((o0, o1, o2, o3)):
        direction = ways[buffer]
        for h in range(slots):
            at = block(lists_out[0, direction * slots + h], size)
            out[0:rows, h * size : (h + 1) * size] = field[:, at]
            out[rows : rows + 8, h * size : (h + 1) * size] = jnp.broadcast_to(
                names[:, at].astype(f32), (8, size)
            )


def split_field(field, wide, size):
    rows, width = field.shape
    high, low = high_low(field[...])
    wide[0:rows, 0:width] = high
    wide[rows : 2 * rows, 0:width] = low
    wide[0 : 2 * rows, width : width + size] = jnp.zeros((2 * rows, size), bf16)


def local_rows(table, lay, matrix, wide, g, size, rows):
    parts = [wide[0:rows, g * size : (g + 1) * size]]
    for k in range(1, lay.count):
        parts.append(wide[0:rows, block(table[lay.columns + g * lay.count + k], size)])
    pieces = [matrix[g * lay.count + k] for k in range(lay.count)]
    return dot_nt(jnp.concatenate(parts, axis=1), jnp.concatenate(pieces, axis=1))


def local_block(table, lay, matrix, wide, g, size, rows):
    return halves(local_rows(table, lay, matrix, wide, g, size, 2 * rows))


def diagonal_row(matrix, same):
    return jnp.sum(jnp.where(same, matrix.astype(f32), 0.0), axis=0, keepdims=True)


def square_mask(size):
    return lax.broadcasted_iota(i32, (size, size), 0) == lax.broadcasted_iota(
        i32, (size, size), 1
    )


def build_table(lists, columns, table, lay):
    ways, there = place_in_mesh()
    for buffer in range(4):
        direction = ways[buffer]
        table[lay.home + direction] = jnp.where(there[buffer], buffer, 4)
        for h in range(lay.slots):
            table[buffer * lay.slots + h] = lists[0, direction * lay.slots + h]
    table[lay.home + 4] = 4
    for buffer in range(5):
        table[lay.counts + buffer] = 0
    for g in range(lay.blocks):
        table[lay.columns + g * lay.count] = columns[0, g]
        for k in range(1, lay.count):
            column = columns[k, g]
            table[lay.columns + g * lay.count + k] = jnp.minimum(column, lay.blocks)
            slot = jnp.maximum(column - lay.blocks, 0)
            direction = jnp.where(column < lay.blocks, 4, lay.direction(slot))
            buffer = table[lay.home + direction]
            found = table[lay.counts + buffer]
            table[lay.entries + buffer * lay.capacity + found] = lay.code(
                g * lay.count + k, g, slot - lay.direction(slot) * lay.slots
            )
            table[lay.counts + buffer] = found + 1
    for buffer in range(4):
        found = table[lay.counts + buffer]
        for i in range(CHUNK):
            table[lay.entries + buffer * lay.capacity + found + i] = lay.slots


def sweep_weights(weights, inverse):
    if weights is None:
        return None, inverse[0:1, :] / center_value
    return weights[0], weights[1] * inverse[0:1, :]


def begin_sweep(left, update, iterate, inverse, new, weights, mode, onehot=None):
    if mode == "restrict":
        new[...] = halves(dot_nt(stacked(left[...]), onehot[...]))
        return
    a, b = sweep_weights(weights, inverse)
    change = b * left[...] if a is None else a * update[...] + b * left[...]
    new[...] = iterate[...] + change if mode == "last" else change


def first_kernel(
    lists, columns, field, target, source, left, new, table, inverse, matrix, wide, right, sems, *, size, lay, parts
):
    per = matrix.shape[0] // parts
    copies = [
        pltpu.make_async_copy(
            source.at[pl.ds(i * per, per)], matrix.at[pl.ds(i * per, per)], sems.at[i]
        )
        for i in range(parts)
    ]
    copies.append(pltpu.make_async_copy(target, right, sems.at[parts]))
    copies[parts].start()
    for copy in copies[:AHEAD]:
        copy.start()
    split_field(field, wide, size)
    build_table(lists, columns, table, lay)
    copies[parts].wait()
    same = square_mask(size)
    for g in range(lay.blocks):
        if g % (lay.blocks // parts) == 0:
            part = g // (lay.blocks // parts)
            copies[part].wait()
            if part + AHEAD < parts:
                copies[part + AHEAD].start()
        at = slice(g * size, (g + 1) * size)
        left[:, at] = right[:, at] - local_block(table, lay, matrix, wide, g, size, left.shape[0])
        inverse[:, at] = jnp.broadcast_to(
            1.0 / diagonal_row(matrix[g * lay.count], same), (8, size)
        )
    begin_sweep(left, None, None, inverse, new, None, "plain")


def local_kernel(table, update, residual, iterate, inverse, matrix, *refs, size, lay, weights, mode):
    refs = list(refs)
    onehot = refs.pop(0) if mode == "restrict" else None
    left, new, iterate_out, wide = refs
    split_field(update, wide, size)
    for g in range(lay.blocks):
        at = slice(g * size, (g + 1) * size)
        left[:, at] = residual[:, at] - local_block(table, lay, matrix, wide, g, size, left.shape[0])
    iterate_out[...] = iterate[...] + update[...]
    begin_sweep(left, update, iterate_out, inverse, new, weights, mode, onehot)


def turn_received(table, lay, matrix, turned, size):
    identity = jnp.where(square_mask(size), 1.0, 0.0).astype(bf16)

    def group(buffer, start):
        for i in range(CHUNK):
            which = table[lay.entries + buffer * lay.capacity + start + i] >> 16
            turned[which] = dot_nt(identity, matrix[which]).astype(bf16)

    for buffer in range(4):
        group(buffer, 0)

        def more(c, carry, buffer=buffer):
            group(buffer, c * CHUNK)
            return carry

        lax.fori_loop(1, (table[lay.counts + buffer] + CHUNK - 1) // CHUNK, more, 0)


def local_and_coarse_kernel(
    table, update, residual, iterate, inverse, matrix, groups, coarse, h0, h1, h2, h3,
    left, new, iterate_out, turned, onehot, cells_turned, names, coarse_high, coarse_low, coarse_inverse, wide, brought, cells, sems, *, size, lay, weights,
):
    copies = [
        pltpu.make_async_copy(coarse, brought, sems.at[0]),
        pltpu.make_async_copy(groups, cells, sems.at[1]),
    ]
    for copy in copies:
        copy.start()
    local_kernel(
        table, update, residual, iterate, inverse, matrix, left, new, iterate_out, wide,
        size=size, lay=lay, weights=weights, mode="plain",
    )
    turn_received(table, lay, matrix, turned, size)
    width = lay.slots * size
    rows = update.shape[0]
    number = lax.broadcasted_iota(i32, (size, width), 0).astype(f32)
    for buffer, received in enumerate((h0, h1, h2, h3)):
        names[:, buffer * width : (buffer + 1) * width] = jnp.where(
            number == received[rows : rows + 1, :], 1.0, 0.0
        ).astype(bf16)
    for copy in copies:
        copy.wait()
    onehot[...] = jnp.where(
        lax.broadcasted_iota(i32, onehot.shape, 0) == cells[...], 1.0, 0.0
    ).astype(bf16)
    identity = jnp.where(square_mask(size), 1.0, 0.0).astype(bf16)
    for g in range(lay.blocks):
        at = slice(g * size, (g + 1) * size)
        cells_turned[at, :] = dot_nt(identity, onehot[:, at]).astype(bf16)
    coarse_inverse[...] = jnp.broadcast_to(
        1.0 / diagonal_row(brought[0], square_mask(size)), (8, size)
    )
    ways, there = place_in_mesh()
    for k in range(5):
        if k == 0:
            piece = brought[0]
        else:
            piece = jnp.where(there[k - 1], brought[1 + ways[k - 1]], 0.0)
        high, low = high_low(piece)
        coarse_high[:, k * size : (k + 1) * size] = high
        coarse_low[:, k * size : (k + 1) * size] = low


def put_halo(wide, place, x, size):
    rows, width = x.shape
    start = place * (width + size)
    high, low = high_low(x)
    wide[0:rows, start : start + width] = high
    wide[rows : 2 * rows, start : start + width] = low
    wide[:, start + width : start + width + size] = jnp.zeros((2 * rows, size), bf16)


def put_halos(wide, halos, buffers, names, rows, lay, size):
    for place, (buffer, received) in enumerate(zip(buffers, halos)):
        x = received[0:rows, :]
        if names is not None:
            width = lay.slots * size
            chosen = names[:, buffer * width : (buffer + 1) * width]
            x = halves(dot_nn(stacked(x), chosen))
        put_halo(wide, place, x, size)


def entry_product(code, matrix, wide, place, lay, size, dot):
    which, row, slot = code >> 16, (code >> 8) & 255, code & 255
    at = block(place * (lay.slots + 1) + slot, size)
    return block(row, size), halves(dot(wide[:, at], matrix[which]))


def for_received(table, lay, buffers, matrix, wide, size, dot, use):
    def group(members):
        use(
            [
                entry_product(
                    table[lay.entries + buffer * lay.capacity + i],
                    matrix, wide, place, lay, size, dot,
                )
                for place, buffer, i in members
            ]
        )

    group([(p, b, i) for p, b in enumerate(buffers) for i in range(CHUNK)])
    for place, buffer in enumerate(buffers):

        def more(c, carry, place=place, buffer=buffer):
            group([(place, buffer, c * CHUNK + i) for i in range(CHUNK)])
            return carry

        chunks = (table[lay.counts + buffer] + CHUNK - 1) // CHUNK
        lax.fori_loop(1, chunks, more, 0)


def received_kernel(table, left_in, new_in, inverse, matrix, *refs, size, lay, weights, mode, buffers, final, turned):
    refs = list(refs)
    halos, refs = refs[: len(buffers)], refs[len(buffers) :]
    rows = left_in.shape[0]
    names = refs.pop(0) if mode == "spread" else None
    if mode == "restrict":
        onehot, coarse_inverse = refs[:2]
        refs = refs[2:]
    wide, scaled = refs[-2:]
    left, new = refs[:2]
    if mode == "last" and final:
        new = refs[0]
        new[...] = new_in[...]
    put_halos(wide, halos, buffers, names, rows, lay, size)
    if mode != "restrict":
        scaled[0:1, :] = sweep_weights(weights, inverse)[1]

    def use(found):
        for at, product in found:
            if mode != "last":
                left[:, at] = left[:, at] - product
            if mode != "restrict":
                new[:, at] = new[:, at] - scaled[0:1, at] * product
        if mode == "restrict":
            new[...] = new[...] - sum(
                halves(dot_nn(stacked(product), onehot[at, :])) for at, product in found
            )

    for_received(table, lay, buffers, matrix, wide, size, dot_nn if turned else dot_nt, use)
    if not final or mode == "last":
        return
    if mode == "restrict":
        refs[2][...] = coarse_inverse[0:1, :] * new[...] / center_value
    else:
        pack(table, new, refs[2:6], size, lay.slots)


def coarse_kernel(
    h0, h1, h2, h3, residual, update, iterate, coarse_high, coarse_low, coarse_inverse, *outs, weights, last
):
    c = update[...]
    rows = c.shape[0]
    received = dict(zip(COARSE, (h0, h1, h2, h3)))
    high, low = high_low(jnp.concatenate([c] + [received[b][...] for b in range(4)], axis=1))
    product = halves(dot_nt(jnp.concatenate([high, low], axis=0), coarse_high[...]))
    left = residual[...] - (product + dot_nt(high, coarse_low[...]))
    new = weights[0] * c + weights[1] * coarse_inverse[0:1, :] * left
    outs[0][...] = iterate[...] + new
    if not last:
        outs[1][...] = left
        outs[2][...] = new


def local_and_spread_kernel(
    table, update, residual, iterate, inverse, matrix, onehot, left, new, iterate_out, high, low, wide, *, size, lay, weights
):
    local_kernel(
        table, update, residual, iterate, inverse, matrix, left, new, iterate_out, wide,
        size=size, lay=lay, weights=weights, mode="plain",
    )
    width = onehot.shape[1]
    wide[0:size, 0:width] = onehot[...]
    wide[0:size, width : width + size] = jnp.zeros((size, size), bf16)
    for g in range(lay.blocks):
        at = slice(g * size, (g + 1) * size)
        high[:, at], low[:, at] = high_low(
            local_rows(table, lay, matrix, wide, g, size, size)
        )


def spread_kernel(
    table, correction, onehot, iterate, leftover, inverse, spread_high, spread_low, left, new, second, correction_out, *, size, lay
):
    rows = correction.shape[0]
    both = stacked(correction[...])
    second[...] = iterate[...] + halves(dot_nn(both, onehot[...]))
    product = halves(dot_nn(both, spread_high[...])) + dot_nn(both[:rows], spread_low[...])
    left[...] = leftover[...] - product
    begin_sweep(left, None, None, inverse, new, None, "plain")
    correction_out[...] = correction[...]


def local_program(
    right_side, start_guess, fine_matrix, fine_columns, send_lists, aggregates, coarse_matrix
):
    perms = exchanges(lax.axis_size("span"), lax.axis_size("stream"))
    rows, width = right_side.shape
    blocks, count, size, _ = fine_matrix.shape
    slots = send_lists.shape[1] // 4
    halo_width = slots * size
    lay = Table(blocks, count, slots)
    groups = aggregates.reshape(1, width)
    stored = fine_matrix.reshape(blocks * count, size, size)
    coarse = coarse_matrix.reshape(coarse_matrix.shape[1:])
    weights = chebyshev_weights()
    parts = 4 if blocks % 4 == 0 else 1

    spaces = {
        "v": pl.BlockSpec(memory_space=pltpu.VMEM),
        "s": pl.BlockSpec(memory_space=pltpu.SMEM),
        "h": pl.BlockSpec(memory_space=pltpu.HBM),
    }

    def call(kernel, ins, outs, scratch=(), where="", kept="", aliases=None, flops=0, **named):
        where = where + "v" * (len(ins) - len(where))
        kept = kept + "v" * (len(outs) - len(kept))
        fixed = {"h": pltpu.HBM, "V": pltpu.VMEM}
        ins = [
            pltpu.with_memory_space_constraint(x, fixed[c]) if c in fixed else x
            for x, c in zip(ins, where)
        ]
        forms = {
            "v": jax.ShapeDtypeStruct,
            "V": pltpu.MemorySpace.VMEM,
            "s": pltpu.MemorySpace.SMEM,
        }
        return pl.pallas_call(
            functools.partial(kernel, **named),
            out_shape=[forms[c](shape, kind) for c, (shape, kind) in zip(kept, outs)],
            in_specs=[spaces[c.lower()] for c in where],
            out_specs=[spaces[c.lower()] for c in kept],
            scratch_shapes=list(scratch),
            input_output_aliases=aliases or {},
            compiler_params=pltpu.CompilerParams(vmem_limit_bytes=VMEM_LIMIT),
            cost_estimate=pl.CostEstimate(
                flops=flops, bytes_accessed=4 * 1024 * 1024, transcendentals=0
            ),
        )(*ins)

    def exchange(payloads):
        return [lax.ppermute(x, AXES, perm) for x, perm in zip(payloads, perms)]

    field = ((rows, width), f32)
    halo = ((rows, halo_width), f32)
    small = ((rows, size), f32)
    wide_local = pltpu.VMEM((2 * rows, width + size), bf16)
    wide_spread = pltpu.VMEM((max(2 * rows, size), width + size), bf16)
    flops = 2 * 2 * rows * blocks * count * size * size
    dims = {"size": size, "lay": lay}

    def received(halos, left, new, weight, mode="plain", extra=()):
        blocks_in = matrix if turned is None else turned
        steps = SPREAD_STEPS if mode == "spread" else STEPS
        for step, buffers in enumerate(steps):
            final = step == len(steps) - 1
            outs, kept = [field, small if mode == "restrict" else field], "VV"
            aliases = {1: 0, 2: 1}
            if mode == "last" and final:
                outs, kept, aliases = [field], "v", None
            elif mode == "restrict" and final:
                outs.append(small)
            elif final:
                outs += [halo] * 4
            result = call(
                received_kernel,
                [table, left, new, inverse, blocks_in] + [halos[b] for b in buffers] + list(extra),
                outs,
                [
                    pltpu.VMEM((2 * rows, len(buffers) * (halo_width + size)), bf16),
                    pltpu.VMEM((8, width), f32),
                ],
                "sVV", kept, aliases, flops=flops * len(buffers) // 20,
                weights=weight, mode=mode, buffers=buffers, final=final,
                turned=turned is not None, **dims,
            )
            left, new = result[0], result[1] if len(result) > 1 else None
        return result

    def local(update, residual, iterate, weight, mode="plain", extra=()):
        return call(
            local_kernel, [table, update, residual, iterate, inverse, matrix] + list(extra),
            [field, small if mode == "restrict" else field, field],
            [wide_local], "s", "VV", flops=flops, weights=weight, mode=mode, **dims,
        )

    *payloads, guess, lists, columns = call(
        load_kernel,
        [start_guess, send_lists, fine_columns.T, groups],
        [((rows + 8, halo_width), f32)] * 4
        + [field, (send_lists.shape, i32), (fine_columns.shape[::-1], i32)],
        [pltpu.VMEM((1, width), i32), pltpu.SemaphoreType.DMA((4,))],
        "hhhh", "vvvvvss", size=size, slots=slots,
    )
    first_halos = halos = exchange(payloads)
    left, new, table, inverse, matrix = call(
        first_kernel,
        [lists, columns, guess, right_side, stored],
        [field, field, ((lay.length,), i32), ((8, width), f32), (stored.shape, bf16)],
        [wide_local, pltpu.VMEM(*field), pltpu.SemaphoreType.DMA((parts + 1,))],
        "ssvhh", "VVs", flops=flops, parts=parts, **dims,
    )
    turned = None
    residual, update, *payloads = received(halos, left, new, None)
    halos = exchange(payloads)
    left, new, iterate, turned, onehot, cells_turned, names, coarse_high, coarse_low, coarse_inverse = call(
        local_and_coarse_kernel,
        [table, update, residual, guess, inverse, matrix, groups, coarse] + first_halos,
        [
            field,
            field,
            field,
            (stored.shape, bf16),
            ((size, width), bf16),
            ((width, size), bf16),
            ((size, 4 * halo_width), bf16),
            ((size, 5 * size), bf16),
            ((size, 5 * size), bf16),
            ((8, size), f32),
        ],
        [
            wide_local,
            pltpu.VMEM(coarse.shape, f32),
            pltpu.VMEM((1, width), i32),
            pltpu.SemaphoreType.DMA((2,)),
        ],
        "svvvvvhh", "VV", flops=flops, weights=weights[0], **dims,
    )
    residual, update, *payloads = received(halos, left, new, weights[0])
    halos = exchange(payloads)
    left, new, iterate, spread_high, spread_low = call(
        local_and_spread_kernel, [table, update, residual, iterate, inverse, matrix, onehot],
        [field, field, field, ((size, width), bf16), ((size, width), bf16)],
        [wide_spread], "s", "VV", flops=flops, weights=weights[1], **dims,
    )
    residual, update, *payloads = received(halos, left, new, weights[1])
    halos = exchange(payloads)
    left, new, iterate = local(update, residual, iterate, None, "restrict", (onehot,))
    leftover, coarse_left, c = received(
        halos, left, new, None, "restrict", (cells_turned, coarse_inverse)
    )
    correction = c
    for i, weight in enumerate(weights):
        halos = exchange([c] * 4)
        result = call(
            coarse_kernel,
            [halos[b] for b in COARSE]
            + [coarse_left, c, correction, coarse_high, coarse_low, coarse_inverse],
            [small] if i == 1 else [small] * 3, weights=weight, last=i == 1,
        )
        correction = result[0]
        if i == 0:
            coarse_left, c = result[1:]
    halos = exchange([correction] * 4)
    left, new, iterate, correction_out = call(
        spread_kernel,
        [table, correction, onehot, iterate, leftover, inverse, spread_high, spread_low],
        [field, field, field, small], (), "s", "VV", flops=flops, **dims,
    )
    residual, update, *payloads = received(halos, left, new, None, "spread", (names,))
    halos = exchange(payloads)
    left, new, iterate = local(update, residual, iterate, weights[0])
    residual, update, *payloads = received(halos, left, new, weights[0])
    halos = exchange(payloads)
    left, new, iterate = local(update, residual, iterate, weights[1], "last")
    result = received(halos, left, new, weights[1], "last")
    return (result[0], correction_out)


def solution(mesh):
    placed = (
        P(None, AXES),
        P(None, AXES),
        P(AXES, None, None, None),
        P(AXES, None),
        P(AXES, None),
        P(AXES),
        P(AXES, None, None, None),
    )
    return jax.shard_map(
        local_program,
        mesh=mesh,
        in_specs=placed,
        out_specs=(P(None, AXES), P(None, AXES)),
        check_vma=False,
    )
```

```python
import functools

import jax
import jax.numpy as jnp
import numpy as np
from jax import lax
from jax.experimental import pallas as pl
from jax.experimental.pallas import tpu as pltpu
from jax.sharding import PartitionSpec as P

center_value = 1.1
radius_value = 0.9
AXES = ("span", "stream")
STEPS = ((0,), (1, 2, 3))
SPREAD_STEPS = ((0,), (3, 2, 1))
AHEAD = 3
COARSE = (3, 2, 1, 0)
CHUNK = 4
VMEM_LIMIT = 16 * 1024 * 1024
f32 = jnp.float32
bf16 = jnp.bfloat16
i32 = jnp.int32


def chebyshev_weights():
    weights = []
    old = radius_value / center_value
    for _ in range(2):
        now = 1.0 / (2.0 * center_value / radius_value - old)
        weights.append((now * old, 2.0 * now / radius_value))
        old = now
    return weights


def directions(s, t, n_span, n_stream, choose):
    span_even, span_odd = choose((s & 1) == 0, 1, 0), choose((s & 1) == 0, 0, 1)
    stream_even, stream_odd = choose((t & 1) == 0, 3, 2), choose((t & 1) == 0, 2, 3)
    end_s = (s == 0) | (s == n_span - 1)
    ahead = (((t + 1) >> 1) & 1) == 0
    return (
        choose(ahead, stream_odd, span_even),
        choose(ahead, span_even, choose(end_s, stream_odd, span_odd)),
        choose(ahead | end_s, span_odd, stream_odd),
        stream_even,
    )


def exchanges(n_span, n_stream):
    steps = ((-1, 0), (1, 0), (0, -1), (0, 1))
    partners = [{} for _ in range(4)]
    for s in range(n_span):
        for t in range(n_stream):
            way = directions(
                np.int32(s), np.int32(t), n_span, n_stream, lambda c, a, b: int(a if c else b)
            )
            for number in range(4):
                other_s, other_t = s + steps[way[number]][0], t + steps[way[number]][1]
                if 0 <= other_s < n_span and 0 <= other_t < n_stream:
                    partners[number][s, t] = (other_s, other_t)
    result = []
    for found in partners:
        idle = [(s, t) for s in range(n_span) for t in range(n_stream) if (s, t) not in found]
        while idle:
            s, t = idle.pop(0)
            other = min(
                idle,
                key=lambda o: (o != (s, t ^ 1), o[0] != s, abs(o[0] - s) + abs(o[1] - t)),
                default=(s, t),
            )
            if other in idle:
                idle.remove(other)
            found[s, t], found[other] = other, (s, t)
        result.append(
            [(s * n_stream + t, o[0] * n_stream + o[1]) for (s, t), o in sorted(found.items())]
        )
    return result


def place_in_mesh():
    s, t = lax.axis_index("span"), lax.axis_index("stream")
    n_span, n_stream = lax.axis_size("span"), lax.axis_size("stream")
    ways = directions(s, t, n_span, n_stream, jnp.where)
    there = [
        jnp.where(
            way < 2,
            jnp.where(way == 0, s > 0, s < n_span - 1),
            jnp.where(way == 2, t > 0, t < n_stream - 1),
        )
        for way in ways
    ]
    return ways, there


def dot_nt(a, b):
    return lax.dot_general(a, b, (((1,), (1,)), ((), ())), preferred_element_type=f32)


def dot_nn(a, b):
    return lax.dot_general(a, b, (((1,), (0,)), ((), ())), preferred_element_type=f32)


def high_low(x):
    high = x.astype(bf16)
    return high, (x - high.astype(f32)).astype(bf16)


def stacked(x):
    return jnp.concatenate(high_low(x), axis=0)


def halves(x):
    rows = x.shape[0] // 2
    return x[:rows] + x[rows:]


def block(index, size):
    return pl.ds(pl.multiple_of(index * size, size), size)


class Table:
    def __init__(self, blocks, count, slots):
        self.blocks, self.count, self.slots = blocks, count, slots
        self.capacity = blocks * (count - 1) + CHUNK
        self.columns = 4 * slots
        self.home = self.columns + blocks * count
        self.counts = self.home + 5
        self.entries = self.counts + 5
        self.length = self.entries + 5 * self.capacity

    def direction(self, slot):
        if self.slots & (self.slots - 1) == 0:
            return slot >> (self.slots.bit_length() - 1)
        return lax.div(slot, self.slots)

    def code(self, which, row, slot):
        return (which << 16) | (row << 8) | slot


def pack(table, field, outs, size, slots):
    for buffer in range(4):
        for h in range(slots):
            source = table[buffer * slots + h]
            outs[buffer][:, h * size : (h + 1) * size] = field[:, block(source, size)]


def load_kernel(
    guess, lists, columns, groups, o0, o1, o2, o3, field, lists_out, columns_out, names, sems, *, size, slots
):
    copies = [
        pltpu.make_async_copy(source, target, sems.at[i])
        for i, (source, target) in enumerate(
            ((lists, lists_out), (guess, field), (groups, names), (columns, columns_out))
        )
    ]
    for copy in copies:
        copy.start()
    ways, _ = place_in_mesh()
    for copy in copies:
        copy.wait()
    rows = field.shape[0]
    for buffer, out in enumerate((o0, o1, o2, o3)):
        direction = ways[buffer]
        for h in range(slots):
            at = block(lists_out[0, direction * slots + h], size)
            out[0:rows, h * size : (h + 1) * size] = field[:, at]
            out[rows : rows + 8, h * size : (h + 1) * size] = jnp.broadcast_to(
                names[:, at].astype(f32), (8, size)
            )


def split_field(field, wide, size):
    rows, width = field.shape
    high, low = high_low(field[...])
    wide[0:rows, 0:width] = high
    wide[rows : 2 * rows, 0:width] = low
    wide[0 : 2 * rows, width : width + size] = jnp.zeros((2 * rows, size), bf16)


def local_rows(table, lay, matrix, wide, g, size, rows):
    parts = [wide[0:rows, g * size : (g + 1) * size]]
    for k in range(1, lay.count):
        parts.append(wide[0:rows, block(table[lay.columns + g * lay.count + k], size)])
    pieces = [matrix[g * lay.count + k] for k in range(lay.count)]
    return dot_nt(jnp.concatenate(parts, axis=1), jnp.concatenate(pieces, axis=1))


def local_block(table, lay, matrix, wide, g, size, rows):
    return halves(local_rows(table, lay, matrix, wide, g, size, 2 * rows))


def diagonal_row(matrix, same):
    return jnp.sum(jnp.where(same, matrix.astype(f32), 0.0), axis=0, keepdims=True)


def square_mask(size):
    return lax.broadcasted_iota(i32, (size, size), 0) == lax.broadcasted_iota(
        i32, (size, size), 1
    )


def build_table(lists, columns, table, lay):
    ways, there = place_in_mesh()
    for buffer in range(4):
        direction = ways[buffer]
        table[lay.home + direction] = jnp.where(there[buffer], buffer, 4)
        for h in range(lay.slots):
            table[buffer * lay.slots + h] = lists[0, direction * lay.slots + h]
    table[lay.home + 4] = 4
    for buffer in range(5):
        table[lay.counts + buffer] = 0
    for g in range(lay.blocks):
        table[lay.columns + g * lay.count] = columns[0, g]
        for k in range(1, lay.count):
            column = columns[k, g]
            table[lay.columns + g * lay.count + k] = jnp.minimum(column, lay.blocks)
            slot = jnp.maximum(column - lay.blocks, 0)
            direction = jnp.where(column < lay.blocks, 4, lay.direction(slot))
            buffer = table[lay.home + direction]
            found = table[lay.counts + buffer]
            table[lay.entries + buffer * lay.capacity + found] = lay.code(
                g * lay.count + k, g, slot - lay.direction(slot) * lay.slots
            )
            table[lay.counts + buffer] = found + 1
    for buffer in range(4):
        found = table[lay.counts + buffer]
        for i in range(CHUNK):
            table[lay.entries + buffer * lay.capacity + found + i] = lay.slots


def sweep_weights(weights, inverse):
    if weights is None:
        return None, inverse[0:1, :] / center_value
    return weights[0], weights[1] * inverse[0:1, :]


def begin_sweep(left, update, iterate, inverse, new, weights, mode, onehot=None):
    if mode == "restrict":
        new[...] = halves(dot_nt(stacked(left[...]), onehot[...]))
        return
    a, b = sweep_weights(weights, inverse)
    change = b * left[...] if a is None else a * update[...] + b * left[...]
    new[...] = iterate[...] + change if mode == "last" else change


def first_kernel(
    lists, columns, field, target, source, left, new, table, inverse, matrix, wide, right, sems, *, size, lay, parts
):
    per = matrix.shape[0] // parts
    copies = [
        pltpu.make_async_copy(
            source.at[pl.ds(i * per, per)], matrix.at[pl.ds(i * per, per)], sems.at[i]
        )
        for i in range(parts)
    ]
    copies.append(pltpu.make_async_copy(target, right, sems.at[parts]))
    copies[parts].start()
    for copy in copies[:AHEAD]:
        copy.start()
    split_field(field, wide, size)
    build_table(lists, columns, table, lay)
    copies[parts].wait()
    same = square_mask(size)
    for g in range(lay.blocks):
        if g % (lay.blocks // parts) == 0:
            part = g // (lay.blocks // parts)
            copies[part].wait()
            if part + AHEAD < parts:
                copies[part + AHEAD].start()
        at = slice(g * size, (g + 1) * size)
        left[:, at] = right[:, at] - local_block(table, lay, matrix, wide, g, size, left.shape[0])
        inverse[:, at] = jnp.broadcast_to(
            1.0 / diagonal_row(matrix[g * lay.count], same), (8, size)
        )
    begin_sweep(left, None, None, inverse, new, None, "plain")


def local_kernel(table, update, residual, iterate, inverse, matrix, *refs, size, lay, weights, mode):
    refs = list(refs)
    onehot = refs.pop(0) if mode == "restrict" else None
    left, new, iterate_out, wide = refs
    split_field(update, wide, size)
    for g in range(lay.blocks):
        at = slice(g * size, (g + 1) * size)
        left[:, at] = residual[:, at] - local_block(table, lay, matrix, wide, g, size, left.shape[0])
    iterate_out[...] = iterate[...] + update[...]
    begin_sweep(left, update, iterate_out, inverse, new, weights, mode, onehot)


def turn_received(table, lay, matrix, turned, size):
    identity = jnp.where(square_mask(size), 1.0, 0.0).astype(bf16)

    def group(buffer, start):
        for i in range(CHUNK):
            which = table[lay.entries + buffer * lay.capacity + start + i] >> 16
            turned[which] = dot_nt(identity, matrix[which]).astype(bf16)

    for buffer in range(4):
        group(buffer, 0)

        def more(c, carry, buffer=buffer):
            group(buffer, c * CHUNK)
            return carry

        lax.fori_loop(1, (table[lay.counts + buffer] + CHUNK - 1) // CHUNK, more, 0)


def local_and_coarse_kernel(
    table, update, residual, iterate, inverse, matrix, groups, coarse, h0, h1, h2, h3,
    left, new, iterate_out, turned, onehot, cells_turned, names, coarse_high, coarse_low, coarse_inverse, wide, brought, cells, sems, *, size, lay, weights,
):
    copies = [
        pltpu.make_async_copy(coarse, brought, sems.at[0]),
        pltpu.make_async_copy(groups, cells, sems.at[1]),
    ]
    for copy in copies:
        copy.start()
    local_kernel(
        table, update, residual, iterate, inverse, matrix, left, new, iterate_out, wide,
        size=size, lay=lay, weights=weights, mode="plain",
    )
    turn_received(table, lay, matrix, turned, size)
    width = lay.slots * size
    rows = update.shape[0]
    number = lax.broadcasted_iota(i32, (size, width), 0).astype(f32)
    for buffer, received in enumerate((h0, h1, h2, h3)):
        names[:, buffer * width : (buffer + 1) * width] = jnp.where(
            number == received[rows : rows + 1, :], 1.0, 0.0
        ).astype(bf16)
    for copy in copies:
        copy.wait()
    onehot[...] = jnp.where(
        lax.broadcasted_iota(i32, onehot.shape, 0) == cells[...], 1.0, 0.0
    ).astype(bf16)
    identity = jnp.where(square_mask(size), 1.0, 0.0).astype(bf16)
    for g in range(lay.blocks):
        at = slice(g * size, (g + 1) * size)
        cells_turned[at, :] = dot_nt(identity, onehot[:, at]).astype(bf16)
    coarse_inverse[...] = jnp.broadcast_to(
        1.0 / diagonal_row(brought[0], square_mask(size)), (8, size)
    )
    ways, there = place_in_mesh()
    for k in range(5):
        if k == 0:
            piece = brought[0]
        else:
            piece = jnp.where(there[k - 1], brought[1 + ways[k - 1]], 0.0)
        high, low = high_low(piece)
        coarse_high[:, k * size : (k + 1) * size] = high
        coarse_low[:, k * size : (k + 1) * size] = low


def put_halo(wide, place, x, size):
    rows, width = x.shape
    start = place * (width + size)
    high, low = high_low(x)
    wide[0:rows, start : start + width] = high
    wide[rows : 2 * rows, start : start + width] = low
    wide[:, start + width : start + width + size] = jnp.zeros((2 * rows, size), bf16)


def put_halos(wide, halos, buffers, names, rows, lay, size):
    for place, (buffer, received) in enumerate(zip(buffers, halos)):
        x = received[0:rows, :]
        if names is not None:
            width = lay.slots * size
            chosen = names[:, buffer * width : (buffer + 1) * width]
            x = halves(dot_nn(stacked(x), chosen))
        put_halo(wide, place, x, size)


def entry_product(code, matrix, wide, place, lay, size, dot):
    which, row, slot = code >> 16, (code >> 8) & 255, code & 255
    at = block(place * (lay.slots + 1) + slot, size)
    return block(row, size), halves(dot(wide[:, at], matrix[which]))


def for_received(table, lay, buffers, matrix, wide, size, dot, use):
    def group(members):
        use(
            [
                entry_product(
                    table[lay.entries + buffer * lay.capacity + i],
                    matrix, wide, place, lay, size, dot,
                )
                for place, buffer, i in members
            ]
        )

    group([(p, b, i) for p, b in enumerate(buffers) for i in range(CHUNK)])
    for place, buffer in enumerate(buffers):

        def more(c, carry, place=place, buffer=buffer):
            group([(place, buffer, c * CHUNK + i) for i in range(CHUNK)])
            return carry

        chunks = (table[lay.counts + buffer] + CHUNK - 1) // CHUNK
        lax.fori_loop(1, chunks, more, 0)


def received_kernel(table, left_in, new_in, inverse, matrix, *refs, size, lay, weights, mode, buffers, final, turned):
    refs = list(refs)
    halos, refs = refs[: len(buffers)], refs[len(buffers) :]
    rows = left_in.shape[0]
    names = refs.pop(0) if mode == "spread" else None
    if mode == "restrict":
        onehot, coarse_inverse = refs[:2]
        refs = refs[2:]
    wide, scaled = refs[-2:]
    left, new = refs[:2]
    if mode == "last" and final:
        new = refs[0]
        new[...] = new_in[...]
    put_halos(wide, halos, buffers, names, rows, lay, size)
    if mode != "restrict":
        scaled[0:1, :] = sweep_weights(weights, inverse)[1]

    def use(found):
        for at, product in found:
            if mode != "last":
                left[:, at] = left[:, at] - product
            if mode != "restrict":
                new[:, at] = new[:, at] - scaled[0:1, at] * product
        if mode == "restrict":
            new[...] = new[...] - sum(
                halves(dot_nn(stacked(product), onehot[at, :])) for at, product in found
            )

    for_received(table, lay, buffers, matrix, wide, size, dot_nn if turned else dot_nt, use)
    if not final or mode == "last":
        return
    if mode == "restrict":
        refs[2][...] = coarse_inverse[0:1, :] * new[...] / center_value
    else:
        pack(table, new, refs[2:6], size, lay.slots)


def coarse_kernel(
    h0, h1, h2, h3, residual, update, iterate, coarse_high, coarse_low, coarse_inverse, *outs, weights, last
):
    c = update[...]
    rows = c.shape[0]
    received = dict(zip(COARSE, (h0, h1, h2, h3)))
    high, low = high_low(jnp.concatenate([c] + [received[b][...] for b in range(4)], axis=1))
    product = halves(dot_nt(jnp.concatenate([high, low], axis=0), coarse_high[...]))
    left = residual[...] - (product + dot_nt(high, coarse_low[...]))
    new = weights[0] * c + weights[1] * coarse_inverse[0:1, :] * left
    outs[0][...] = iterate[...] + new
    if not last:
        outs[1][...] = left
        outs[2][...] = new


def local_and_spread_kernel(
    table, update, residual, iterate, inverse, matrix, onehot, left, new, iterate_out, high, low, wide, *, size, lay, weights
):
    local_kernel(
        table, update, residual, iterate, inverse, matrix, left, new, iterate_out, wide,
        size=size, lay=lay, weights=weights, mode="plain",
    )
    width = onehot.shape[1]
    wide[0:size, 0:width] = onehot[...]
    wide[0:size, width : width + size] = jnp.zeros((size, size), bf16)
    for g in range(lay.blocks):
        at = slice(g * size, (g + 1) * size)
        high[:, at], low[:, at] = high_low(
            local_rows(table, lay, matrix, wide, g, size, size)
        )


def spread_kernel(
    table, correction, onehot, iterate, leftover, inverse, spread_high, spread_low, left, new, second, correction_out, *, size, lay
):
    rows = correction.shape[0]
    both = stacked(correction[...])
    second[...] = iterate[...] + halves(dot_nn(both, onehot[...]))
    product = halves(dot_nn(both, spread_high[...])) + dot_nn(both[:rows], spread_low[...])
    left[...] = leftover[...] - product
    begin_sweep(left, None, None, inverse, new, None, "plain")
    correction_out[...] = correction[...]


def local_program(
    right_side, start_guess, fine_matrix, fine_columns, send_lists, aggregates, coarse_matrix
):
    perms = exchanges(lax.axis_size("span"), lax.axis_size("stream"))
    rows, width = right_side.shape
    blocks, count, size, _ = fine_matrix.shape
    slots = send_lists.shape[1] // 4
    halo_width = slots * size
    lay = Table(blocks, count, slots)
    groups = aggregates.reshape(1, width)
    stored = fine_matrix.reshape(blocks * count, size, size)
    coarse = coarse_matrix.reshape(coarse_matrix.shape[1:])
    weights = chebyshev_weights()
    parts = 4 if blocks % 4 == 0 else 1

    spaces = {
        "v": pl.BlockSpec(memory_space=pltpu.VMEM),
        "s": pl.BlockSpec(memory_space=pltpu.SMEM),
        "h": pl.BlockSpec(memory_space=pltpu.HBM),
    }

    def call(kernel, ins, outs, scratch=(), where="", kept="", aliases=None, flops=0, **named):
        where = where + "v" * (len(ins) - len(where))
        kept = kept + "v" * (len(outs) - len(kept))
        fixed = {"h": pltpu.HBM, "V": pltpu.VMEM}
        ins = [
            pltpu.with_memory_space_constraint(x, fixed[c]) if c in fixed else x
            for x, c in zip(ins, where)
        ]
        forms = {
            "v": jax.ShapeDtypeStruct,
            "V": pltpu.MemorySpace.VMEM,
            "s": pltpu.MemorySpace.SMEM,
        }
        return pl.pallas_call(
            functools.partial(kernel, **named),
            out_shape=[forms[c](shape, kind) for c, (shape, kind) in zip(kept, outs)],
            in_specs=[spaces[c.lower()] for c in where],
            out_specs=[spaces[c.lower()] for c in kept],
            scratch_shapes=list(scratch),
            input_output_aliases=aliases or {},
            compiler_params=pltpu.CompilerParams(vmem_limit_bytes=VMEM_LIMIT),
            cost_estimate=pl.CostEstimate(
                flops=flops, bytes_accessed=4 * 1024 * 1024, transcendentals=0
            ),
        )(*ins)

    def exchange(payloads):
        return [lax.ppermute(x, AXES, perm) for x, perm in zip(payloads, perms)]

    field = ((rows, width), f32)
    halo = ((rows, halo_width), f32)
    small = ((rows, size), f32)
    wide_local = pltpu.VMEM((2 * rows, width + size), bf16)
    wide_spread = pltpu.VMEM((max(2 * rows, size), width + size), bf16)
    flops = 2 * 2 * rows * blocks * count * size * size
    dims = {"size": size, "lay": lay}

    def received(halos, left, new, weight, mode="plain", extra=()):
        blocks_in = matrix if turned is None else turned
        steps = SPREAD_STEPS if mode == "spread" else STEPS
        for step, buffers in enumerate(steps):
            final = step == len(steps) - 1
            outs, kept = [field, small if mode == "restrict" else field], "VV"
            aliases = {1: 0, 2: 1}
            if mode == "last" and final:
                outs, kept, aliases = [field], "v", None
            elif mode == "restrict" and final:
                outs.append(small)
            elif final:
                outs += [halo] * 4
            result = call(
                received_kernel,
                [table, left, new, inverse, blocks_in] + [halos[b] for b in buffers] + list(extra),
                outs,
                [
                    pltpu.VMEM((2 * rows, len(buffers) * (halo_width + size)), bf16),
                    pltpu.VMEM((8, width), f32),
                ],
                "sVV", kept, aliases, flops=flops * len(buffers) // 20,
                weights=weight, mode=mode, buffers=buffers, final=final,
                turned=turned is not None, **dims,
            )
            left, new = result[0], result[1] if len(result) > 1 else None
        return result

    def local(update, residual, iterate, weight, mode="plain", extra=()):
        return call(
            local_kernel, [table, update, residual, iterate, inverse, matrix] + list(extra),
            [field, small if mode == "restrict" else field, field],
            [wide_local], "s", "VVV", flops=flops, weights=weight, mode=mode, **dims,
        )

    *payloads, guess, lists, columns = call(
        load_kernel,
        [start_guess, send_lists, fine_columns.T, groups],
        [((rows + 8, halo_width), f32)] * 4
        + [field, (send_lists.shape, i32), (fine_columns.shape[::-1], i32)],
        [pltpu.VMEM((1, width), i32), pltpu.SemaphoreType.DMA((4,))],
        "hhhh", "vvvvvss", size=size, slots=slots,
    )
    first_halos = halos = exchange(payloads)
    left, new, table, inverse, matrix = call(
        first_kernel,
        [lists, columns, guess, right_side, stored],
        [field, field, ((lay.length,), i32), ((8, width), f32), (stored.shape, bf16)],
        [wide_local, pltpu.VMEM(*field), pltpu.SemaphoreType.DMA((parts + 1,))],
        "ssvhh", "VVs", flops=flops, parts=parts, **dims,
    )
    turned = None
    residual, update, *payloads = received(halos, left, new, None)
    halos = exchange(payloads)
    left, new, iterate, turned, onehot, cells_turned, names, coarse_high, coarse_low, coarse_inverse = call(
        local_and_coarse_kernel,
        [table, update, residual, guess, inverse, matrix, groups, coarse] + first_halos,
        [
            field,
            field,
            field,
            (stored.shape, bf16),
            ((size, width), bf16),
            ((width, size), bf16),
            ((size, 4 * halo_width), bf16),
            ((size, 5 * size), bf16),
            ((size, 5 * size), bf16),
            ((8, size), f32),
        ],
        [
            wide_local,
            pltpu.VMEM(coarse.shape, f32),
            pltpu.VMEM((1, width), i32),
            pltpu.SemaphoreType.DMA((2,)),
        ],
        "svvvvvhh", "VV", flops=flops, weights=weights[0], **dims,
    )
    residual, update, *payloads = received(halos, left, new, weights[0])
    halos = exchange(payloads)
    left, new, iterate, spread_high, spread_low = call(
        local_and_spread_kernel, [table, update, residual, iterate, inverse, matrix, onehot],
        [field, field, field, ((size, width), bf16), ((size, width), bf16)],
        [wide_spread], "s", "VV", flops=flops, weights=weights[1], **dims,
    )
    residual, update, *payloads = received(halos, left, new, weights[1])
    halos = exchange(payloads)
    left, new, iterate = local(update, residual, iterate, None, "restrict", (onehot,))
    leftover, coarse_left, c = received(
        halos, left, new, None, "restrict", (cells_turned, coarse_inverse)
    )
    correction = c
    for i, weight in enumerate(weights):
        halos = exchange([c] * 4)
        result = call(
            coarse_kernel,
            [halos[b] for b in COARSE]
            + [coarse_left, c, correction, coarse_high, coarse_low, coarse_inverse],
            [small] if i == 1 else [small] * 3, weights=weight, last=i == 1,
        )
        correction = result[0]
        if i == 0:
            coarse_left, c = result[1:]
    halos = exchange([correction] * 4)
    left, new, iterate, correction_out = call(
        spread_kernel,
        [table, correction, onehot, iterate, leftover, inverse, spread_high, spread_low],
        [field, field, field, small], (), "s", "VV", flops=flops, **dims,
    )
    residual, update, *payloads = received(halos, left, new, None, "spread", (names,))
    halos = exchange(payloads)
    left, new, iterate = local(update, residual, iterate, weights[0])
    residual, update, *payloads = received(halos, left, new, weights[0])
    halos = exchange(payloads)
    left, new, iterate = local(update, residual, iterate, weights[1], "last")
    result = received(halos, left, new, weights[1], "last")
    return (result[0], correction_out)


def solution(mesh):
    placed = (
        P(None, AXES),
        P(None, AXES),
        P(AXES, None, None, None),
        P(AXES, None),
        P(AXES, None),
        P(AXES),
        P(AXES, None, None, None),
    )
    return jax.shard_map(
        local_program,
        mesh=mesh,
        in_specs=placed,
        out_specs=(P(None, AXES), P(None, AXES)),
        check_vma=False,
    )
```
